512 devices in a mesh: dp: 128 (over z, y, core), split: 4 (over x).
Axes of the slice: x: 4, y: 8, z: 8, core: 2. Of those that a mesh axis runs over, the one named last changes fastest.
Arguments:
- tokens: bfloat16 [65536, 1024], P(('dp', 'split')), may hold values from -6 to 6
- w_up: bfloat16 [1024, 2048], P('dp', 'split'), may hold values from -0.1875 to 0.1875
- b_up: bfloat16 [2048], P('split'), may hold values from -3 to 3
- w_down: bfloat16 [2048, 1024], P('split', 'dp'), may hold values from -0.125 to 0.125
- ln_gain: float32 [1024], replicated, may hold values from 0.5 to 2
- doc_lengths: int32 [512, 16], P(('dp', 'split')), may hold values from 1 to 64, 128 in all within a row
- pool_rows: bfloat16 [57344, 1024], P(('dp', 'split')), may hold values from -12 to 12
- cluster_ids: int32 [65536], P(('dp', 'split')), may hold values from 0 to 511, as said below
Outputs:
- best_similarity: float32 [65536], P(('dp', 'split'))
The draws below stay inside these ranges and needn't reach their ends.
Inputs may be any that keep to these rules, and one draw needn't show every extreme that they name: `cluster_ids`: cluster c belongs to owner c mod 128. The 128 rows of one device hold at most 2 rows of the clusters of any one owner; in every draw one owner gets exactly 2 rows from every device.
All inputs are finite; a program needn't handle non-finite values.
Results may differ from the reference program's by a relative error of at most 0.00046.
Values may be sent and summed in bfloat16 or wider, within the bound.
A program may use at most 64 MiB of HBM per device.

```python
import math
import jax
import jax.numpy as jnp
import numpy as np
from jax import lax

D = 1024
FF = 2048
TOK_DEV = 128
DOC_DEV = 16
ROW_DEV = 128
CL_OWN = 4
MOST_LEN = 64
POOL_DEV = 112
OWNERS = 128
CAP = 2
CLUSTERS = 512
TOKENS = 65536
POOL_ROWS = 57344
ROWS = 65536
DEVICES = 512


def layout_ids(key):
    slot_count = OWNERS * CAP
    heavy = (jax.random.randint(jax.random.fold_in(key, 7), (OWNERS,), 0, 4) == 0).astype(jnp.int32)
    forced = jax.random.randint(jax.random.fold_in(key, 8), (), 0, OWNERS)
    slot_owner = jnp.arange(slot_count, dtype=jnp.int32) // CAP

    def one_device(device):
        dev_key = jax.random.fold_in(key, device + 100)
        noise_low = jax.random.randint(jax.random.fold_in(dev_key, 1), (slot_count,), 0, 4096)
        priority = 2 * (slot_owner == forced).astype(jnp.int32) + heavy[slot_owner]
        scores = (priority * 4096 + noise_low) * slot_count + jnp.arange(slot_count, dtype=jnp.int32)
        chosen = jnp.argsort(-scores)[:ROW_DEV]
        owners = jax.random.permutation(jax.random.fold_in(dev_key, 2), slot_owner[chosen])
        draws = jax.random.randint(jax.random.fold_in(dev_key, 3), (ROW_DEV,), 0, CL_OWN + 2)
        within = jnp.maximum(draws - 2, 0)
        return owners + OWNERS * within
    return jax.vmap(one_device)(jnp.arange(DEVICES, dtype=jnp.int32)).reshape(ROWS).astype(jnp.int32)


def draw_cluster_ids(key, part):
    return layout_ids(key)


def draw_pool_rows(key, part):
    labels = layout_ids(key).reshape(DEVICES, ROW_DEV)[:, :POOL_DEV].reshape(POOL_ROWS)
    centres = jax.random.normal(jax.random.fold_in(key, 21), (CLUSTERS, D), jnp.float32)
    centre_rows = centres[labels]
    spread = jnp.exp(jax.random.uniform(jax.random.fold_in(key, 22), (POOL_ROWS, 1), jnp.float32, jnp.log(0.3), jnp.log(3.0)))
    noise = jax.random.normal(jax.random.fold_in(key, 23), (POOL_ROWS, D), jnp.float32)
    values = centre_rows + spread * noise
    return jnp.clip(values, -12.0, 12.0).astype(jnp.bfloat16)


def block_scale(own_key, extent, pieces, smallest, top_value):
    factor_of = 1.0
    for axis_at, blocks in pieces:
        heights = jax.random.uniform(jax.random.fold_in(jax.random.fold_in(own_key, 6), axis_at), (blocks,), jnp.float32, smallest / len(pieces), top_value / len(pieces))
        factor_of = factor_of * jnp.repeat(jnp.exp(heights), extent[axis_at] // blocks).reshape((-1,) + (1,) * (len(extent) - 1 - axis_at))
    return factor_of


def split_up(number_of, total, bound, skew):
    portions = [(1 << 20) // math.isqrt(grade ** skew) + 1 for grade in range(2, number_of + 1)]
    rest, counts = total - bound - (number_of - 1), [1] * (number_of - 1)
    while rest > 0:
        candidates = [i for i in range(number_of - 1) if counts[i] < bound]
        whole, remaining = sum([portions[i] for i in candidates]), rest
        for i in candidates:
            extra = min(bound - counts[i], max(1, remaining * portions[i] // whole), rest)
            counts[i] = counts[i] + extra
            rest = rest - extra
    return np.array([bound] + counts)


def uneven(stream_key, count, total, bound, slope):
    if count == 2:
        one = jax.random.randint(stream_key, (), max(1, total - bound), min(bound, total - 1) + 1)
        return jnp.stack([one, total - one])
    sizes = jnp.asarray(split_up(count, total, bound, slope), jnp.int32)
    pairs = (count - 1) // 2
    source_of, taker = sizes[1:1 + 2 * pairs:2], sizes[2:2 + 2 * pairs:2]
    room = jnp.minimum(source_of - 1, bound - taker)
    shifted = jax.random.randint(jax.random.fold_in(stream_key, 1), (pairs,), 0, 1 << 20) % (room + 1)
    sizes = sizes.at[1:1 + 2 * pairs:2].set(source_of - shifted).at[2:2 + 2 * pairs:2].set(taker + shifted)
    return sizes[jax.random.permutation(jax.random.fold_in(stream_key, 2), count)]


def scatter_about(key, shape, scale, most, pieces=(), kind=jnp.bfloat16):
    gain = block_scale(key, shape, pieces, -0.22, 0.18) if pieces else 1.0
    values = jax.random.normal(key, shape, jnp.float32) * scale * gain
    return jnp.minimum(jnp.maximum(values, -most), most).astype(kind)


def setup_inputs(seed: int = 0) -> dict:
    key_list = jax.random.split(jax.random.key(seed), 9)
    tokens = scatter_about(key_list[0], (TOKENS, D), 1.0, 6.0, ((0, 512),))
    w_up = scatter_about(key_list[1], (D, FF), D ** -0.5, 0.1875, ((0, 128), (1, 4)))
    b_up = scatter_about(key_list[2], (FF,), 0.5, 3.0, ((0, 4),))
    w_down = scatter_about(key_list[3], (FF, D), FF ** -0.5, 0.125, ((0, 4), (1, 128)))
    ln_gain = jnp.clip(jnp.exp(jax.random.uniform(key_list[4], (D,), jnp.float32, math.log(0.5), math.log(2.0))), 0.5, 2.0)
    doc_lengths = jax.vmap(lambda own: uneven(own, DOC_DEV, TOK_DEV, MOST_LEN, 2))(jax.random.split(key_list[5], DEVICES)).reshape((DEVICES, DOC_DEV)).astype(jnp.int32)
    pool_rows = draw_pool_rows(jax.random.fold_in(key_list[8], 71), 0)
    cluster_ids = draw_cluster_ids(jax.random.fold_in(key_list[8], 71), 0)
    return {"tokens": tokens, "w_up": w_up, "b_up": b_up, "w_down": w_down, "ln_gain": ln_gain, "doc_lengths": doc_lengths, "pool_rows": pool_rows, "cluster_ids": cluster_ids}


def unit_rows(values):
    return (values * lax.rsqrt(lax.optimization_barrier(jnp.sum(values * values, axis=1, keepdims=True)) + 1e-06)).astype(jnp.bfloat16)

def reference(tokens, w_up, b_up, w_down, ln_gain, doc_lengths, pool_rows, cluster_ids):

    def encode(items):
        tok_rows, lengths = items
        pre_act = jnp.dot(tok_rows, w_up, preferred_element_type=jnp.float32) + b_up.astype(jnp.float32)
        hidden = jax.nn.gelu(pre_act, approximate=False).astype(jnp.bfloat16)
        state = tok_rows.astype(jnp.float32) + jnp.dot(hidden, w_down, preferred_element_type=jnp.float32)
        mean_row = lax.optimization_barrier(jnp.mean(state, axis=1, keepdims=True))
        centred = state - mean_row
        var_row = lax.optimization_barrier(jnp.mean(centred * centred, axis=1, keepdims=True))
        normed = centred * lax.rsqrt(var_row + 1e-05) * ln_gain[None, :]
        ends = jnp.cumsum(lengths)
        begins = ends - lengths
        places = jnp.arange(TOK_DEV, dtype=jnp.int32)
        member = ((places[None, :] >= begins[:, None]) & (places[None, :] < ends[:, None])).astype(jnp.float32)
        pooled = jnp.dot(member, normed, precision=lax.Precision.HIGHEST) / lengths[:, None].astype(jnp.float32)
        return unit_rows(pooled)
    fresh = lax.map(encode, (tokens.reshape(DEVICES, TOK_DEV, D), doc_lengths))
    earlier = unit_rows(pool_rows.astype(jnp.float32)).reshape(DEVICES, POOL_DEV, D)
    emb = jnp.concatenate([earlier, fresh], axis=1).reshape(ROWS, D)
    margin = DEVICES * CAP
    order = jnp.argsort(cluster_ids, stable=True).astype(jnp.int32)
    sorted_rows = emb[order]
    sorted_ids = cluster_ids[order]
    padded_rows = jnp.concatenate([jnp.zeros((margin, D), jnp.bfloat16), sorted_rows, jnp.zeros((margin, D), jnp.bfloat16)], axis=0)
    padded_ids = jnp.concatenate([jnp.full((margin,), -1, jnp.int32), sorted_ids, jnp.full((margin,), -1, jnp.int32)], axis=0)
    width = ROW_DEV + 2 * margin

    def block(index):
        low = (index * ROW_DEV).astype(jnp.int32)
        queries = lax.dynamic_slice_in_dim(sorted_rows, low, ROW_DEV, 0)
        query_ids = lax.dynamic_slice_in_dim(sorted_ids, low, ROW_DEV, 0)
        window = lax.dynamic_slice_in_dim(padded_rows, low, width, 0)
        window_ids = lax.dynamic_slice_in_dim(padded_ids, low, width, 0)
        scores = lax.dot_general(queries, window, (((1,), (1,)), ((), ())), preferred_element_type=jnp.float32)
        columns = jnp.arange(width, dtype=jnp.int32)
        rows_at = jnp.arange(ROW_DEV, dtype=jnp.int32)
        keep = (query_ids[:, None] == window_ids[None, :]) & (columns[None, :] != rows_at[:, None] + margin)
        return lax.optimization_barrier(jnp.max(jnp.where(keep, scores, jnp.float32(-1.0)), axis=1))
    sorted_best = lax.map(block, jnp.arange(DEVICES, dtype=jnp.int32)).reshape(ROWS)
    return jnp.zeros((ROWS,), jnp.float32).at[order].set(sorted_best)
```

```python
import functools
import math

import jax
import jax.numpy as jnp
from jax import lax
from jax.experimental import pallas as pl
from jax.experimental.pallas import tpu as pltpu
from jax.sharding import PartitionSpec as P

MESH = pl.DeviceIdType.MESH
F32, BF16 = jnp.float32, jnp.bfloat16
LAB = 128


def iota(shape, dim):
    return lax.broadcasted_iota(jnp.int32, shape, dim)


def mm(a, b):
    return jnp.dot(a, b, preferred_element_type=F32)


def mm_nt(a, b):
    return lax.dot_general(a, b, (((1,), (1,)), ((), ())), preferred_element_type=F32)


def unit_rows(v):
    return (v * lax.rsqrt(jnp.sum(v * v, axis=1, keepdims=True) + 1e-06)).astype(BF16)


def here(n):
    me = lax.axis_index("dp")
    return me, me // (2 * n), (me // 2) % n, me % 2, lax.axis_index("split")


def to_column(row, size):
    eye = iota((size, size), 0) == iota((size, size), 1)
    return jnp.sum(jnp.where(eye, row, 0.0), axis=1, keepdims=True)


def slots(ids_ref, n):
    dp = 2 * n * n
    rows = ids_ref.shape[1]
    ids = ids_ref[...]
    owner, label = ids & (dp - 1), ids >> int(math.log2(dp))
    owner_col = to_column(owner.astype(F32), rows)
    same = owner_col == owner.astype(F32)
    before = iota((rows, rows), 0) < iota((rows, rows), 1)
    place = jnp.sum(jnp.where(same & before, 1.0, 0.0), axis=0, keepdims=True).astype(jnp.int32)
    return owner, place, to_column(label.astype(F32), rows)


def remote(src, dst, send, recv, dev):
    return pltpu.make_async_remote_copy(
        src_ref=src, dst_ref=dst, send_sem=send, recv_sem=recv, device_id=dev, device_id_type=MESH
    )


def encode_kernel(
    n, nx, shard, tok, bias, gain, lengths, pool, ids, s0, s1,
    G, T, up, down, PS, RF, RA, emb,
    lsem, p1s, p1r, rs_, rr, sibs, sibr, ts, tr, fs, fr, qs, qr,
):
    me, z, y, c, x = here(n)
    hh = shard.shape[2]
    toks, d = tok.shape
    half = toks // 2
    xp, xm = (x + 1) % nx, (x + nx - 1) % nx
    xo = (x + 2) % nx
    place = (y, z)

    def at_z(zz):
        return ((zz * n + y) * 2 + c, x)

    def at_y(yy):
        return ((z * n + yy) * 2 + c, x)

    ring = (at_y, at_z)
    first = (at_z, at_y)
    sibling = (me + 1 - 2 * c, x)

    barrier = pltpu.get_barrier_semaphore()

    @pl.loop(1, n)
    def _(k):
        pl.semaphore_signal(barrier, 1, device_id=at_z((z + k) % n), device_id_type=MESH)
        pl.semaphore_signal(barrier, 1, device_id=at_y((y + k) % n), device_id_type=MESH)

    pl.semaphore_signal(barrier, 1, device_id=sibling, device_id_type=MESH)
    pl.semaphore_signal(barrier, 1, device_id=(me, xp), device_id_type=MESH)
    pl.semaphore_signal(barrier, 1, device_id=(me, xm), device_id_type=MESH)
    pl.semaphore_wait(barrier, 2 * (n - 1) + 3)

    lo, hi = pl.ds(0, half), pl.ds(half, half)

    own0 = pltpu.make_async_copy(shard.at[0], G.at[c, 0, y, z], lsem.at[0])
    own1 = pltpu.make_async_copy(shard.at[1], G.at[c, 1, z, y], lsem.at[1])
    own0.start()
    own1.start()

    def first_hop(h, k):
        mine = (z, y)[h]
        other = (mine + k) % n
        slot = G.at[c, 0, y, z] if h == 0 else G.at[c, 1, z, y]
        return remote(shard.at[h], slot, p1s.at[h, other], p1r.at[h, mine], first[h](other))

    @pl.loop(1, n)
    def _(k):
        first_hop(0, k).start()
        first_hop(1, k).start()

    t_send = [
        remote(tok.at[lo], T.at[x, lo], ts.at[0], tr.at[0], (me, xp)),
        remote(tok.at[hi], T.at[x, hi], ts.at[1], tr.at[1], (me, xm)),
        remote(tok.at[hi], T.at[x, hi], ts.at[2], tr.at[2], (me, xp)),
        remote(tok.at[lo], T.at[x, lo], ts.at[3], tr.at[3], (me, xm)),
    ]
    for t in t_send:
        t.start()

    pool_n = pool.shape[0]
    emb[0:pool_n, :] = unit_rows(pool[...].astype(F32))

    own0.wait()
    own1.wait()

    @pl.loop(1, n)
    def _(k):
        for h in range(2):
            mine = (z, y)[h]
            other = (mine + k) % n
            slot = G.at[c, 0, y, other] if h == 0 else G.at[c, 1, z, other]
            remote(shard.at[h], slot, p1s.at[h, other], p1r.at[h, other], first[h](other)).wait_recv()

    last = n // 2 - 1
    hops, sib = [], []

    def to_sibling(h, i, k):
        cp = remote(G.at[c, h, i], G.at[c, h, i], sibs.at[h, k], sibr.at[h, k], sibling)
        cp.start()
        sib.append(cp)

    for s in range(n // 2):
        for h in range(2):
            q = place[h]
            a, b = (q + n - s) % n, (q + s) % n
            if s:
                hops[-4 if h == 0 else -4][0].wait_recv()
                hops[-3 if h == 0 else -3][0].wait_recv()
                to_sibling(h, a, 2 * s - 1)
                to_sibling(h, b, 2 * s)
            else:
                to_sibling(h, q, 0)
            ra, rb = G.at[c, h, a], G.at[c, h, b]
            if s == last:
                ra, rb = G.at[c, h, a, pl.ds(0, n // 2)], G.at[c, h, b, pl.ds(n // 2, n // 2)]
            cp = remote(ra, ra, rs_.at[0, h, s], rr.at[0, h, s], ring[h]((q + 1) % n))
            cm = remote(rb, rb, rs_.at[1, h, s], rr.at[1, h, s], ring[h]((q + n - 1) % n))
            cp.start()
            cm.start()
            hops += [(cp,), (cm,)]

    t_send[0].wait_recv()
    f0 = remote(T.at[xm, lo], T.at[xm, lo], fs.at[0], fr.at[0], (me, xp))
    f0.start()
    t_send[1].wait_recv()
    f1 = remote(T.at[xp, hi], T.at[xp, hi], fs.at[1], fr.at[1], (me, xm))
    f1.start()

    for h in range(2):
        hops[-4 + 2 * h][0].wait_recv()
        hops[-3 + 2 * h][0].wait_recv()
        to_sibling(h, (place[h] + n // 2) % n, n - 1)

    owner, place_in, label_col = slots(ids, n)
    dp = 2 * n * n
    rows = ids.shape[1]
    lane_slot = iota((2 * dp, rows), 0)
    target0 = ((owner % (2 * n)) * n + owner // (2 * n)) * 2 + place_in
    target1 = owner * 2 + place_in
    pick0 = jnp.where(lane_slot == target0, 1.0, 0.0).astype(BF16)
    pick1 = jnp.where(lane_slot == target1, 1.0, 0.0).astype(BF16)
    lab = jnp.broadcast_to(label_col + 1.0, (rows, LAB)).astype(BF16)
    s0[:, d // 2 :] = mm(pick0, lab).astype(BF16)

    for cp in sib:
        cp.wait_recv()

    m = n * 16
    o, i_ = iota((2 * m, 2 * m), 0), iota((2 * m, 2 * m), 1)
    w_, rest = o // m, o % m
    n_, c_, r_ = rest // 16, (rest // 8) % 2, rest % 8
    order = jnp.where(i_ == c_ * m + n_ * 16 + w_ * 8 + r_, 1.0, 0.0).astype(BF16)

    @pl.loop(0, n)
    def _(i):
        for h in range(2):
            both = jnp.concatenate([G[0, h, i].reshape(m, hh), G[1, h, i].reshape(m, hh)], axis=0)
            w = mm(order, both).astype(BF16)
            cols = slice(h * hh, (h + 1) * hh)
            for ref, part in ((up, w[:m]), (down, w[m:])):
                if h == 0:
                    for zz in range(n):
                        at = pl.multiple_of((zz * n + i) * 16, 16)
                        ref[pl.ds(at, 16), cols] = part[zz * 16 : (zz + 1) * 16]
                else:
                    ref[pl.ds(pl.multiple_of(i * m, m), m), cols] = part

    def ffn(block):
        pre = mm(block, up[...]) + bias[...].astype(F32)
        hidden = (0.5 * pre * (1.0 + lax.erf(pre * (0.5**0.5)))).astype(BF16)
        return mm_nt(hidden, down[...])

    for t in t_send[2:]:
        t.wait_recv()
    f0.wait_recv()
    f1.wait_recv()
    PS[0] = ffn(T[xo]).astype(BF16)
    q0 = remote(PS.at[0, lo], RF.at[0], qs.at[0], qr.at[0], (me, xp))
    q1 = remote(PS.at[0, hi], RF.at[1], qs.at[1], qr.at[1], (me, xm))
    q0.start()
    q1.start()
    right = ffn(T[xp])
    PS[1, hi] = right[half:].astype(BF16)
    q2 = remote(PS.at[1, hi], RA.at[0, hi], qs.at[2], qr.at[2], (me, xp))
    q2.start()
    left = ffn(T[xm])
    PS[2, lo] = left[:half].astype(BF16)
    q3 = remote(PS.at[2, lo], RA.at[1, lo], qs.at[3], qr.at[3], (me, xm))
    q3.start()
    q0.wait_recv()
    PS[1, lo] = (right[:half] + RF[0].astype(F32)).astype(BF16)
    q4 = remote(PS.at[1, lo], RA.at[0, lo], qs.at[4], qr.at[4], (me, xp))
    q4.start()
    q1.wait_recv()
    PS[2, hi] = (left[half:] + RF[1].astype(F32)).astype(BF16)
    q5 = remote(PS.at[2, hi], RA.at[1, hi], qs.at[5], qr.at[5], (me, xm))
    q5.start()
    state = tok[...].astype(F32) + ffn(tok[...])
    for q in (q2, q3, q4, q5):
        q.wait_recv()
    state = state + RA[0].astype(F32) + RA[1].astype(F32)

    mean = jnp.mean(state, axis=1, keepdims=True)
    centred = state - mean
    var = jnp.mean(centred * centred, axis=1, keepdims=True)
    normed = centred * lax.rsqrt(var + 1e-05) * gain[...]
    docs = lengths.shape[1]
    len_row = lengths[...].astype(F32)
    len_col = to_column(len_row, docs)
    upto = iota((docs, docs), 1) <= iota((docs, docs), 0)
    ends = jnp.sum(jnp.where(upto, len_row, 0.0), axis=1, keepdims=True)
    places = iota((docs, toks), 1).astype(F32)
    member = jnp.where((places >= ends - len_col) & (places < ends), 1.0, 0.0)
    pooled = (
        jnp.dot(member, normed, precision=lax.Precision.HIGHEST, preferred_element_type=F32)
        / len_col
    )
    emb[pool_n : pool_n + docs, :] = unit_rows(pooled)

    s0[:, : d // 2] = mm(pick0, emb[:, : d // 2]).astype(BF16)
    s1[...] = mm(pick1, emb[:, d // 2 :]).astype(BF16)

    @pl.loop(1, n)
    def _(k):
        first_hop(0, k).wait_send()
        first_hop(1, k).wait_send()

    for cp in [*t_send, f0, f1, q0, q1, q2, q3, q4, q5, *[h[0] for h in hops], *sib]:
        cp.wait_send()


def search_kernel(
    n, nx, s0, s1, ids, out,
    R0, T0, F0, R1, T1, F1, E, LR, MX, GX, B1, B2, B3,
    lsem, s0s, s0r, s1s, s1r, t0s, t0r, t1s, t1r, es, er, ms, mr, b1s, b1r, b2s, b2r,
):
    me, z, y, c, x = here(n)
    yc = me % (2 * n)
    nyc = 2 * n
    w0 = s0.shape[2]
    w1 = s1.shape[2]
    total = 2 * nyc * n
    xp, xm = (x + 1) % nx, (x + nx - 1) % nx

    def at_z(zz):
        return (zz * nyc + yc, x)

    def at_yc(other):
        return (z * nyc + other, x)

    barrier = pltpu.get_barrier_semaphore()

    @pl.loop(1, n)
    def _(k):
        pl.semaphore_signal(barrier, 1, device_id=at_z((z + k) % n), device_id_type=MESH)

    @pl.loop(1, nyc)
    def _(k):
        pl.semaphore_signal(barrier, 1, device_id=at_yc((yc + k) % nyc), device_id_type=MESH)

    pl.semaphore_signal(barrier, 1, device_id=(me, xp), device_id_type=MESH)
    pl.semaphore_signal(barrier, 1, device_id=(me, xm), device_id_type=MESH)
    pl.semaphore_wait(barrier, n + nyc)

    def all_to_all(src, dst, mine, count, dev, send, recv, local):
        own = pltpu.make_async_copy(src.at[mine], dst.at[mine], local)

        def to(k):
            other = (mine + k) % count
            return remote(src.at[other], dst.at[mine], send.at[other], recv.at[mine], dev(other))

        def start():
            own.start()

            @pl.loop(1, count)
            def _(k):
                to(k).start()

        def wait():
            @pl.loop(1, count)
            def _(k):
                other = (mine + k) % count
                remote(src.at[other], dst.at[other], send.at[other], recv.at[other], dev(other)).wait()

            own.wait()

        return start, wait

    def spread(src, dst, mine, count, dev, send, recv, local):
        own = pltpu.make_async_copy(src, dst.at[mine], local)

        def start():
            own.start()

            @pl.loop(1, count)
            def _(k):
                other = (mine + k) % count
                remote(src, dst.at[mine], send.at[other], recv.at[mine], dev(other)).start()

        def wait():
            @pl.loop(1, count)
            def _(k):
                other = (mine + k) % count
                remote(src, dst.at[other], send.at[other], recv.at[other], dev(other)).wait()

            own.wait()

        return start, wait

    a0 = all_to_all(s0, R0, yc, nyc, at_yc, s0s, s0r, lsem.at[0])
    a1 = all_to_all(s1, R1, z, n, at_z, s1s, s1r, lsem.at[1])
    b0 = all_to_all(T0, F0, z, n, at_z, t0s, t0r, lsem.at[2])
    b1 = all_to_all(T1, F1, yc, nyc, at_yc, t1s, t1r, lsem.at[3])
    a0[0]()
    a1[0]()

    row, col = iota((total, total), 0), iota((total, total), 1)
    z_, yc_, s_ = row // (2 * nyc), (row // 2) % nyc, row % 2
    by_z = jnp.where(col == (yc_ * n + z_) * 2 + s_, 1.0, 0.0).astype(BF16)
    yc_, z_ = row // (2 * n), (row // 2) % n
    by_yc = jnp.where(col == (z_ * nyc + yc_) * 2 + s_, 1.0, 0.0).astype(BF16)

    a0[1]()
    T0[...] = mm(by_z, R0[...].reshape(total, w0)).astype(BF16).reshape(n, 2 * nyc, w0)
    b0[0]()
    a1[1]()
    T1[...] = mm(by_yc, R1[...].reshape(total, w1)).astype(BF16).reshape(nyc, 2 * n, w1)
    b1[0]()
    b0[1]()
    E[0, :, w1:] = F0[...].reshape(total, w0)
    b1[1]()
    E[0, :, :w1] = mm(by_z, F1[...].reshape(total, w1)).astype(BF16)

    to_p = remote(E.at[0], E.at[1], es.at[0], er.at[0], (me, xp))
    to_m = remote(E.at[0], E.at[2], es.at[1], er.at[1], (me, xm))
    to_p.start()
    to_m.start()

    d = w0 - LAB + w1
    eye = row == col

    def labels(i):
        col_ = E[i, :, d : d + 1].astype(F32)
        return col_, jnp.sum(jnp.where(eye, col_, 0.0), axis=0, keepdims=True)

    def best_of(rows_from, lab_col, cols_from, lab_row, self_too):
        sc = mm_nt(E[rows_from, :, :d], E[cols_from, :, :d])
        keep = lab_col == lab_row
        if self_too:
            keep = keep & ~eye
        return jnp.max(jnp.where(keep, sc, -1.0), axis=0, keepdims=True)

    col0, row0 = labels(0)
    best = best_of(0, col0, 0, row0, True)
    to_p.wait_recv()
    to_m.wait_recv()
    col1, row1 = labels(1)
    col2, _ = labels(2)
    MX[...] = jnp.broadcast_to(best_of(2, col2, 1, row1, False), MX.shape)
    mx = remote(MX, GX, ms.at[0], mr.at[0], (me, xm))
    mx.start()
    best = jnp.maximum(best, best_of(1, col1, 0, row0, False))
    best = jnp.maximum(best, best_of(2, col2, 0, row0, False))
    owner, place_in, _ = slots(ids, n)
    mx.wait_recv()
    B1[...] = jnp.broadcast_to(jnp.maximum(best, GX[0:1, :]), B1.shape)

    c1 = spread(B1.at[pl.ds(0, 1)], B2, z, n, at_z, b1s, b1r, lsem.at[4])
    c1[0]()
    c1[1]()
    LR[...] = B2[...].reshape(n, total)
    c2 = spread(LR, B3, yc, nyc, at_yc, b2s, b2r, lsem.at[5])
    c2[0]()
    c2[1]()
    got = B3[...].reshape(nyc * n, total)
    lane = iota((nyc * n, total), 1)
    v0 = jnp.sum(jnp.where(lane == me * 2, got, 0.0), axis=1, keepdims=True)
    v1 = jnp.sum(jnp.where(lane == me * 2 + 1, got, 0.0), axis=1, keepdims=True)
    rows = ids.shape[1]
    mine = iota((nyc * n, rows), 0) == (owner % nyc) * n + owner // nyc
    out[...] = jnp.sum(jnp.where(mine, jnp.where(place_in == 0, v0, v1), 0.0), axis=0, keepdims=True)
    to_p.wait_send()
    to_m.wait_send()
    mx.wait_send()


VM = pl.BlockSpec(memory_space=pltpu.VMEM)
DMA = pltpu.SemaphoreType.DMA


def on_device(n, nx, tokens, w_up, b_up, w_down, ln_gain, doc_lengths, pool_rows, cluster_ids):
    toks, d = tokens.shape
    hid = w_up.shape[1]
    hh = hid // 2
    rows = cluster_ids.shape[0]
    dp = 2 * n * n
    shard = jnp.concatenate([w_up, w_down.T], axis=0)
    shard = jnp.stack([shard[:, :hh], shard[:, hh:]])
    ids = cluster_ids.reshape(1, rows)
    params = functools.partial(
        pltpu.CompilerParams, has_side_effects=True, vmem_limit_bytes=50 * 2**20
    )
    w0, w1 = d // 2 + LAB, d // 2
    s0, s1 = pl.pallas_call(
        functools.partial(encode_kernel, n, nx),
        out_shape=[
            jax.ShapeDtypeStruct((2 * dp, w0), BF16),
            jax.ShapeDtypeStruct((2 * dp, w1), BF16),
        ],
        in_specs=[VM] * 7,
        out_specs=[VM] * 2,
        scratch_shapes=[
            pltpu.VMEM((2, 2, n, n, 16, hh), BF16),
            pltpu.VMEM((nx, toks, d), BF16),
            pltpu.VMEM((d, hid), BF16),
            pltpu.VMEM((d, hid), BF16),
            pltpu.VMEM((3, toks, d), BF16),
            pltpu.VMEM((2, toks // 2, d), BF16),
            pltpu.VMEM((2, toks, d), BF16),
            pltpu.VMEM((rows, d), BF16),
            DMA((2,)),
            DMA((2, n)),
            DMA((2, n)),
            DMA((2, 2, n)),
            DMA((2, 2, n)),
            DMA((2, n)),
            DMA((2, n)),
            DMA((4,)),
            DMA((4,)),
            DMA((2,)),
            DMA((2,)),
            DMA((6,)),
            DMA((6,)),
        ],
        compiler_params=params(collective_id=0),
    )(
        shard,
        tokens,
        b_up.reshape(1, hid),
        ln_gain.reshape(1, d),
        doc_lengths,
        pool_rows,
        ids,
    )
    nyc = 2 * n
    out = pl.pallas_call(
        functools.partial(search_kernel, n, nx),
        out_shape=jax.ShapeDtypeStruct((1, rows), F32),
        in_specs=[VM] * 3,
        out_specs=VM,
        scratch_shapes=[
            pltpu.VMEM((nyc, 2 * n, w0), BF16),
            pltpu.VMEM((n, 2 * nyc, w0), BF16),
            pltpu.VMEM((n, 2 * nyc, w0), BF16),
            pltpu.VMEM((n, 2 * nyc, w1), BF16),
            pltpu.VMEM((nyc, 2 * n, w1), BF16),
            pltpu.VMEM((nyc, 2 * n, w1), BF16),
            pltpu.VMEM((3, 2 * dp, w0 + w1), BF16),
            pltpu.VMEM((n, 2 * dp), F32),
            pltpu.VMEM((8, 2 * dp), F32),
            pltpu.VMEM((8, 2 * dp), F32),
            pltpu.VMEM((8, 2 * dp), F32),
            pltpu.VMEM((n, 1, 2 * dp), F32),
            pltpu.VMEM((nyc, n, 2 * dp), F32),
            DMA((6,)),
            DMA((nyc,)),
            DMA((nyc,)),
            DMA((n,)),
            DMA((n,)),
            DMA((n,)),
            DMA((n,)),
            DMA((nyc,)),
            DMA((nyc,)),
            DMA((2,)),
            DMA((2,)),
            DMA((1,)),
            DMA((1,)),
            DMA((n,)),
            DMA((n,)),
            DMA((nyc,)),
            DMA((nyc,)),
        ],
        compiler_params=params(collective_id=1),
    )(s0.reshape(nyc, 2 * n, w0), s1.reshape(n, 2 * nyc, w1), ids)
    return out.reshape(rows)


def solution(mesh):
    n = math.isqrt(mesh.shape["dp"] // 2)
    placed = (
        P(("dp", "split"), None),
        P("dp", "split"),
        P("split"),
        P("split", "dp"),
        P(),
        P(("dp", "split"), None),
        P(("dp", "split"), None),
        P(("dp", "split")),
    )
    return jax.shard_map(
        functools.partial(on_device, n, mesh.shape["split"]),
        mesh=mesh,
        in_specs=placed,
        out_specs=P(("dp", "split")),
        check_vma=False,
    )
```

```python
import functools
import math

import jax
import jax.numpy as jnp
from jax import lax
from jax.experimental import pallas as pl
from jax.experimental.pallas import tpu as pltpu
from jax.sharding import PartitionSpec as P

MESH = pl.DeviceIdType.MESH
F32, BF16 = jnp.float32, jnp.bfloat16
LAB = 128


def iota(shape, dim):
    return lax.broadcasted_iota(jnp.int32, shape, dim)


def mm(a, b):
    return jnp.dot(a, b, preferred_element_type=F32)


def mm_nt(a, b):
    return lax.dot_general(a, b, (((1,), (1,)), ((), ())), preferred_element_type=F32)


def unit_rows(v):
    return (v * lax.rsqrt(jnp.sum(v * v, axis=1, keepdims=True) + 1e-06)).astype(BF16)


def here(n):
    me = lax.axis_index("dp")
    return me, me // (2 * n), (me // 2) % n, me % 2, lax.axis_index("split")


def to_column(row, size):
    eye = iota((size, size), 0) == iota((size, size), 1)
    return jnp.sum(jnp.where(eye, row, 0.0), axis=1, keepdims=True)


def slots(ids_ref, n):
    dp = 2 * n * n
    rows = ids_ref.shape[1]
    ids = ids_ref[...]
    owner, label = ids & (dp - 1), ids >> int(math.log2(dp))
    owner_col = to_column(owner.astype(F32), rows)
    same = owner_col == owner.astype(F32)
    before = iota((rows, rows), 0) < iota((rows, rows), 1)
    place = jnp.sum(jnp.where(same & before, 1.0, 0.0), axis=0, keepdims=True).astype(jnp.int32)
    return owner, place, to_column(label.astype(F32), rows)


def remote(src, dst, send, recv, dev):
    return pltpu.make_async_remote_copy(
        src_ref=src, dst_ref=dst, send_sem=send, recv_sem=recv, device_id=dev, device_id_type=MESH
    )


def exchange(src, dst, mine, count, dev, send, recv, spread=False):
    def piece(other):
        return src if spread else src.at[other]

    def start():
        @pl.loop(1, count)
        def _(k):
            other = (mine + k) % count
            remote(piece(other), dst.at[mine], send.at[other], recv.at[mine], dev(other)).start()

        dst[mine] = src[...] if spread else src[mine]

    def wait():
        @pl.loop(1, count)
        def _(k):
            other = (mine + k) % count
            remote(piece(other), dst.at[other], send.at[other], recv.at[other], dev(other)).wait()

    return start, wait


def kernel(
    n, nx, tok_in, w_up, w_down, bias, gain, lengths, pool_in, ids, out,
    tok, pool, shard, G, T, up, down, PS, RA, emb,
    SL, RL, TL, L, SP, RP, TP, FP, SQ, RQ, TQ, FQ, E, B1, B2, BM, LR, B3,
    lsem, p1s, p1r, ws, wr, sibs, sibr, ts, tr, qs, qr,
    yls, ylr, zls, zlr, lxs, lxr, yps, ypr, zps, zpr, zqs, zqr, yqs, yqr, es, er,
    b1s, b1r, bms, bmr, b2s, b2r,
):
    me, z, y, c, x = here(n)
    nyc = 2 * n
    yc = me % nyc
    dp = nyc * n
    total = 2 * dp
    hh = shard.shape[2]
    toks, d = tok.shape
    rows = ids.shape[1]
    xp, xm, xo = (x + 1) % nx, (x + nx - 1) % nx, (x + 2) % nx

    def at_z(zz):
        return (zz * nyc + yc, x)

    def at_y(yy):
        return ((z * n + yy) * 2 + c, x)

    def at_yc(other):
        return (z * nyc + other, x)

    place = (y, z)
    ring = (at_y, at_z)
    first = (at_z, at_y)
    sibling = (me + 1 - 2 * c, x)

    load_tok = pltpu.make_async_copy(tok_in, tok, lsem.at[0])
    load_pool = pltpu.make_async_copy(pool_in, pool, lsem.at[1])
    load_tok.start()
    load_pool.start()

    barrier = pltpu.get_barrier_semaphore()

    def greet(dev):
        pl.semaphore_signal(barrier, 1, device_id=dev, device_id_type=MESH)

    @pl.loop(1, n)
    def _(k):
        zz = (z + k) % n
        greet(at_z(zz))
        greet((zz * nyc + yc, xp))

    @pl.loop(1, nyc)
    def _(k):
        greet(at_yc((yc + k) % nyc))

    for other in (xp, xm, xo):
        greet((me, other))

    both = jnp.concatenate([w_up[...].astype(F32), w_down[...].astype(F32)], axis=0).astype(BF16)
    shard[0] = both[:, :hh]
    shard[1] = both[:, hh:]
    load_tok.wait()
    pl.semaphore_wait(barrier, 2 * (n - 1) + nyc - 1 + 3)

    def first_hop(h, k):
        mine = (z, y)[h]
        other = (mine + k) % n
        slot = G.at[c, 0, y, z] if h == 0 else G.at[c, 1, z, y]
        return remote(shard.at[h], slot, p1s.at[h, other], p1r.at[h, mine], first[h](other))

    @pl.loop(1, n)
    def _(k):
        first_hop(0, k).start()
        first_hop(1, k).start()

    t_send = [
        remote(tok, T.at[0], ts.at[0], tr.at[0], (me, xp)),
        remote(tok, T.at[1], ts.at[1], tr.at[1], (me, xm)),
        remote(tok, T.at[2], ts.at[2], tr.at[2], (me, xo)),
    ]
    for t in t_send:
        t.start()
    G[c, 0, y, z] = shard[0]
    G[c, 1, z, y] = shard[1]

    owner, place_in, label_col = slots(ids, n)
    slot = iota((total, rows), 0)
    target0 = ((owner % nyc) * n + owner // nyc) * 2 + place_in
    target1 = owner * 2 + place_in
    pick0 = jnp.where(slot == target0, 1.0, 0.0).astype(BF16)
    pick1 = jnp.where(slot == target1, 1.0, 0.0).astype(BF16)
    lab = jnp.broadcast_to(label_col + 1.0, (rows, LAB)).astype(BF16)
    SL[...] = mm(pick0, lab).astype(BF16).reshape(nyc, 2 * n, LAB)
    lab_y = exchange(SL, RL, yc, nyc, at_yc, yls, ylr)
    lab_z = exchange(TL, L.at[0], z, n, at_z, zls, zlr)
    lab_y[0]()

    @pl.loop(1, n)
    def _(k):
        for h in range(2):
            mine = (z, y)[h]
            other = (mine + k) % n
            slot_ = G.at[c, 0, y, other] if h == 0 else G.at[c, 1, z, other]
            remote(shard.at[h], slot_, p1s.at[h, other], p1r.at[h, other], first[h](other)).wait_recv()

    def second_hop(h, k):
        q = place[h]
        other = (q + k) % n
        return remote(G.at[c, h, q], G.at[c, h, q], ws.at[h, other], wr.at[h, q], ring[h](other))

    def to_sibling(h, i):
        return remote(G.at[c, h, i], G.at[c, h, i], sibs.at[h, i], sibr.at[h, i], sibling)

    @pl.loop(1, n)
    def _(k):
        second_hop(0, k).start()
        second_hop(1, k).start()

    to_sibling(0, y).start()
    to_sibling(1, z).start()

    load_pool.wait()
    pool_n = pool.shape[0]
    emb[0:pool_n, :] = unit_rows(pool[...].astype(F32))

    row, col = iota((total, total), 0), iota((total, total), 1)
    z_, yc_, s_ = row // (2 * nyc), (row // 2) % nyc, row % 2
    by_z = jnp.where(col == (yc_ * n + z_) * 2 + s_, 1.0, 0.0).astype(BF16)
    yc_, z_ = row // (2 * n), (row // 2) % n
    by_yc = jnp.where(col == (z_ * nyc + yc_) * 2 + s_, 1.0, 0.0).astype(BF16)
    eye = row == col
    lab_y[1]()
    TL[...] = mm(by_z, RL[...].reshape(total, LAB)).astype(BF16).reshape(n, 2 * nyc, LAB)
    lab_z[0]()

    @pl.loop(1, n)
    def _(k):
        for h in range(2):
            other = (place[h] + k) % n
            g = G.at[c, h, other]
            remote(g, g, ws.at[h, other], wr.at[h, other], ring[h](other)).wait_recv()
            to_sibling(h, other).start()

    lab_z[1]()
    lx = [
        remote(L.at[0], L.at[1], lxs.at[0], lxr.at[0], (me, xp)),
        remote(L.at[0], L.at[2], lxs.at[1], lxr.at[1], (me, xm)),
    ]
    for t in lx:
        t.start()

    m = n * 16
    o, i_ = iota((2 * m, 2 * m), 0), iota((2 * m, 2 * m), 1)
    w_, rest = o // m, o % m
    n_, c_, r_ = rest // 16, (rest // 8) % 2, rest % 8
    order = jnp.where(i_ == c_ * m + n_ * 16 + w_ * 8 + r_, 1.0, 0.0).astype(BF16)

    @pl.loop(0, n)
    def _(i):
        for h in range(2):
            g = G.at[1 - c, h, i]
            remote(g, g, sibs.at[h, i], sibr.at[h, i], sibling).wait_recv()

    @pl.loop(0, n)
    def _(i):
        for h in range(2):
            pair = jnp.concatenate([G[0, h, i].reshape(m, hh), G[1, h, i].reshape(m, hh)], axis=0)
            w = mm(order, pair).astype(BF16)
            cols = slice(h * hh, (h + 1) * hh)
            for ref, part in ((up, w[:m]), (down, w[m:])):
                if h == 0:
                    for zz in range(n):
                        at = pl.multiple_of((zz * n + i) * 16, 16)
                        ref[pl.ds(at, 16), cols] = part[zz * 16 : (zz + 1) * 16]
                else:
                    ref[pl.ds(pl.multiple_of(i * m, m), m), cols] = part

    def ffn(block):
        pre = mm(block, up[...]) + bias[...].astype(F32)
        hidden = (0.5 * pre * (1.0 + lax.erf(pre * (0.5**0.5)))).astype(BF16)
        return mm_nt(hidden, down[...])

    sums = []
    for j, (held, to) in enumerate(((2, xo), (1, xp), (0, xm))):
        t_send[held].wait_recv()
        PS[j] = ffn(T[held]).astype(BF16)
        sums.append(remote(PS.at[j], RA.at[j], qs.at[j], qr.at[j], (me, to)))
        sums[-1].start()
    state = tok[...].astype(F32) + ffn(tok[...])
    for q in sums:
        q.wait_recv()
    for j in range(3):
        state = state + RA[j].astype(F32)

    mean = jnp.mean(state, axis=1, keepdims=True)
    centred = state - mean
    var = jnp.mean(centred * centred, axis=1, keepdims=True)
    normed = centred * lax.rsqrt(var + 1e-05) * gain[...]
    docs = lengths.shape[1]
    len_row = lengths[...].astype(F32)
    len_col = to_column(len_row, docs)
    upto = iota((docs, docs), 1) <= iota((docs, docs), 0)
    ends = jnp.sum(jnp.where(upto, len_row, 0.0), axis=1, keepdims=True)
    places = iota((docs, toks), 1).astype(F32)
    member = jnp.where((places >= ends - len_col) & (places < ends), 1.0, 0.0)
    pooled = (
        jnp.dot(member, normed, precision=lax.Precision.HIGHEST, preferred_element_type=F32)
        / len_col
    )
    emb[pool_n : pool_n + docs, :] = unit_rows(pooled)

    w = d // 4
    p_y = [exchange(SP.at[k], RP.at[k], yc, nyc, at_yc, yps.at[k], ypr.at[k]) for k in range(2)]
    p_z = [exchange(TP.at[k], FP.at[k], z, n, at_z, zps.at[k], zpr.at[k]) for k in range(2)]
    q_z = [exchange(SQ.at[k], RQ.at[k], z, n, at_z, zqs.at[k], zqr.at[k]) for k in range(2)]
    q_y = [exchange(TQ.at[k], FQ.at[k], yc, nyc, at_yc, yqs.at[k], yqr.at[k]) for k in range(2)]
    for k in range(2):
        e0 = emb[:, 2 * k * w : (2 * k + 1) * w]
        e1 = emb[:, (2 * k + 1) * w : (2 * k + 2) * w]
        SP[k] = mm(pick0, e0).astype(BF16).reshape(nyc, 2 * n, w)
        p_y[k][0]()
        SQ[k] = mm(pick1, e1).astype(BF16).reshape(n, 2 * nyc, w)
        q_z[k][0]()
    for k in range(2):
        p_y[k][1]()
        TP[k] = mm(by_z, RP[k].reshape(total, w)).astype(BF16).reshape(n, 2 * nyc, w)
        p_z[k][0]()
        q_z[k][1]()
        TQ[k] = mm(by_yc, RQ[k].reshape(total, w)).astype(BF16).reshape(nyc, 2 * n, w)
        q_y[k][0]()

    xs = []
    for k in range(2):
        p_z[k][1]()
        E[0, k, :, :w] = FP[k].reshape(total, w)
        q_y[k][1]()
        E[0, k, :, w:] = mm(by_z, FQ[k].reshape(total, w)).astype(BF16)
        xs.append(remote(E.at[0, k], E.at[1, k], es.at[0, k], er.at[0, k], (me, xp)))
        xs.append(remote(E.at[0, k], E.at[2, k], es.at[1, k], er.at[1, k], (me, xm)))
        xs[-2].start()
        xs[-1].start()

    for t in lx:
        t.wait_recv()

    def labels(i):
        column = L[i].reshape(total, LAB)[:, 0:1].astype(F32)
        return column, jnp.sum(jnp.where(eye, column, 0.0), axis=0, keepdims=True)

    (col0, row0), (col1, row1), (col2, _) = labels(0), labels(1), labels(2)

    def part(j, i, k):
        return mm_nt(E[j, k], E[i, k])

    def best_of(sc, keep):
        return jnp.max(jnp.where(keep, sc, -1.0), axis=0, keepdims=True)

    best = best_of(part(0, 0, 0) + part(0, 0, 1), (col0 == row0) & ~eye)
    xs[0].wait_recv()
    xs[1].wait_recv()
    s21, s10, s20 = part(2, 1, 0), part(1, 0, 0), part(2, 0, 0)
    xs[2].wait_recv()
    xs[3].wait_recv()
    B1[1] = jnp.broadcast_to(best_of(s21 + part(2, 1, 1), col2 == row1), B1.shape[1:])
    over = B1.at[1, pl.ds(0, 1)]

    @pl.loop(0, n)
    def _(zz):
        remote(over, BM.at[z], bms.at[zz], bmr.at[z], (zz * nyc + yc, xm)).start()

    best = jnp.maximum(best, best_of(s10 + part(1, 0, 1), col1 == row0))
    best = jnp.maximum(best, best_of(s20 + part(2, 0, 1), col2 == row0))
    B1[0] = jnp.broadcast_to(best, B1.shape[1:])

    back_z = exchange(B1.at[0, pl.ds(0, 1)], B2, z, n, at_z, b1s, b1r, spread=True)
    back_z[0]()

    @pl.loop(0, n)
    def _(zz):
        remote(over, BM.at[zz], bms.at[zz], bmr.at[zz], (zz * nyc + yc, xm)).wait()

    back_z[1]()
    both_ = jnp.maximum(B2[...], BM[...]).reshape(n, total)
    LR[...] = pltpu.roll(both_, (total - z * 2 * nyc) % total, 1)[:, : LR.shape[1]]
    back_y = exchange(LR, B3, yc, nyc, at_yc, b2s, b2r, spread=True)
    back_y[0]()
    back_y[1]()
    got = B3[...].reshape(dp, LR.shape[1])
    lane = iota(got.shape, 1)
    v0 = jnp.sum(jnp.where(lane == yc * 2, got, 0.0), axis=1, keepdims=True)
    v1 = jnp.sum(jnp.where(lane == yc * 2 + 1, got, 0.0), axis=1, keepdims=True)
    mine = iota((dp, rows), 0) == (owner % nyc) * n + owner // nyc
    out[...] = jnp.sum(jnp.where(mine, jnp.where(place_in == 0, v0, v1), 0.0), axis=0, keepdims=True)

    @pl.loop(1, n)
    def _(k):
        for h in range(2):
            first_hop(h, k).wait_send()
            second_hop(h, k).wait_send()

    @pl.loop(0, n)
    def _(i):
        to_sibling(0, i).wait_send()
        to_sibling(1, i).wait_send()

    for t in [*t_send, *sums, *lx, *xs]:
        t.wait_send()


VM = pl.BlockSpec(memory_space=pltpu.VMEM)
ANY = pl.BlockSpec(memory_space=pl.ANY)


def on_device(n, nx, tokens, w_up, b_up, w_down, ln_gain, doc_lengths, pool_rows, cluster_ids):
    toks, d = tokens.shape
    hid = w_up.shape[1]
    hh = hid // 2
    rows = cluster_ids.shape[0]
    nyc = 2 * n
    dp = nyc * n
    total = 2 * dp
    w = d // 4
    keep = min(total, 128)

    def vm(*shape):
        return pltpu.VMEM(shape, BF16)

    def vf(*shape):
        return pltpu.VMEM(shape, F32)

    def two(*shape):
        return [pltpu.SemaphoreType.DMA(shape)] * 2

    out = pl.pallas_call(
        functools.partial(kernel, n, nx),
        out_shape=jax.ShapeDtypeStruct((1, rows), F32),
        in_specs=[ANY, VM, VM, VM, VM, VM, ANY, VM],
        out_specs=VM,
        scratch_shapes=[
            vm(toks, d),
            vm(*pool_rows.shape),
            vm(2, 16, hh),
            vm(2, 2, n, n, 16, hh),
            vm(3, toks, d),
            vm(d, hid),
            vm(d, hid),
            vm(3, toks, d),
            vm(3, toks, d),
            vm(rows, d),
            vm(nyc, 2 * n, LAB),
            vm(nyc, 2 * n, LAB),
            vm(n, 2 * nyc, LAB),
            vm(3, n, 2 * nyc, LAB),
            vm(2, nyc, 2 * n, w),
            vm(2, nyc, 2 * n, w),
            vm(2, n, 2 * nyc, w),
            vm(2, n, 2 * nyc, w),
            vm(2, n, 2 * nyc, w),
            vm(2, n, 2 * nyc, w),
            vm(2, nyc, 2 * n, w),
            vm(2, nyc, 2 * n, w),
            vm(3, 2, total, 2 * w),
            vf(2, 8, total),
            vf(n, 1, total),
            vf(n, 1, total),
            vf(n, keep),
            vf(nyc, n, keep),
            pltpu.SemaphoreType.DMA((2,)),
            *two(2, n),
            *two(2, n),
            *two(2, n),
            *two(3),
            *two(3),
            *two(nyc),
            *two(n),
            *two(2),
            *two(2, nyc),
            *two(2, n),
            *two(2, n),
            *two(2, nyc),
            *two(2, 2),
            *two(n),
            *two(n),
            *two(nyc),
        ],
        compiler_params=pltpu.CompilerParams(
            collective_id=0, has_side_effects=True, vmem_limit_bytes=58 * 2**20
        ),
    )(
        tokens,
        w_up,
        w_down.T,
        b_up.reshape(1, hid),
        ln_gain.reshape(1, d),
        doc_lengths,
        pool_rows,
        cluster_ids.reshape(1, rows),
    )
    return out.reshape(rows)


def solution(mesh):
    n = math.isqrt(mesh.shape["dp"] // 2)
    placed = (
        P(("dp", "split"), None),
        P("dp", "split"),
        P("split"),
        P("split", "dp"),
        P(),
        P(("dp", "split"), None),
        P(("dp", "split"), None),
        P(("dp", "split")),
    )
    return jax.shard_map(
        functools.partial(on_device, n, mesh.shape["split"]),
        mesh=mesh,
        in_specs=placed,
        out_specs=P(("dp", "split")),
        check_vma=False,
    )
```

```python
import functools
import math

import jax
import jax.numpy as jnp
from jax import lax
from jax.experimental import pallas as pl
from jax.experimental.pallas import tpu as pltpu
from jax.sharding import PartitionSpec as P

MESH = pl.DeviceIdType.MESH
F32, BF16 = jnp.float32, jnp.bfloat16
LAB = 128


def iota(shape, dim):
    return lax.broadcasted_iota(jnp.int32, shape, dim)


def mm(a, b):
    return jnp.dot(a, b, preferred_element_type=F32)


def mm_nt(a, b):
    return lax.dot_general(a, b, (((1,), (1,)), ((), ())), preferred_element_type=F32)


def unit_rows(v):
    return (v * lax.rsqrt(jnp.sum(v * v, axis=1, keepdims=True) + 1e-06)).astype(BF16)


def here(n):
    me = lax.axis_index("dp")
    return me, me // (2 * n), (me // 2) % n, me % 2, lax.axis_index("split")


def to_column(row, size):
    eye = iota((size, size), 0) == iota((size, size), 1)
    return jnp.sum(jnp.where(eye, row, 0.0), axis=1, keepdims=True)


def slots(ids_ref, n):
    dp = 2 * n * n
    rows = ids_ref.shape[1]
    ids = ids_ref[...]
    owner, label = ids & (dp - 1), ids >> int(math.log2(dp))
    owner_col = to_column(owner.astype(F32), rows)
    same = owner_col == owner.astype(F32)
    before = iota((rows, rows), 0) < iota((rows, rows), 1)
    place = jnp.sum(jnp.where(same & before, 1.0, 0.0), axis=0, keepdims=True).astype(jnp.int32)
    return owner, place, to_column(label.astype(F32), rows)


def remote(src, dst, send, recv, dev):
    return pltpu.make_async_remote_copy(
        src_ref=src, dst_ref=dst, send_sem=send, recv_sem=recv, device_id=dev, device_id_type=MESH
    )


def exchange(src, dst, mine, count, dev, send, recv, spread=False):
    def piece(other):
        return src if spread else src.at[other]

    def start():
        @pl.loop(1, count)
        def _(k):
            other = (mine + k) % count
            remote(piece(other), dst.at[mine], send.at[other], recv.at[mine], dev(other)).start()

        dst[mine] = src[...] if spread else src[mine]

    def wait():
        @pl.loop(1, count)
        def _(k):
            other = (mine + k) % count
            remote(piece(other), dst.at[other], send.at[other], recv.at[other], dev(other)).wait()

    return start, wait


def kernel(
    n, nx, tok_in, w_up_in, w_down_in, bias_in, gain_in, lengths_in, pool_in, ids_in, out,
    tok, w_up, w_down, bias, gain, lengths, pool, ids, shard, G, T, up, down, PS, RA, RF, emb,
    SL, RL, TL, L, SP, RP, TP, FP, SQ, RQ, TQ, FQ, E, B1, B2, BM, LR, B3,
    lsem, p1s, p1r, ws, wr, sibs, sibr, ts, tr, qs, qr,
    yls, ylr, zls, zlr, lxs, lxr, yps, ypr, zps, zpr, zqs, zqr, yqs, yqr, es, er,
    b1s, b1r, bms, bmr, b2s, b2r,
):
    me, z, y, c, x = here(n)
    nyc = 2 * n
    yc = me % nyc
    dp = nyc * n
    total = 2 * dp
    hh = shard.shape[2]
    toks, d = tok.shape
    rows = ids.shape[1]
    xp, xm, xo = (x + 1) % nx, (x + nx - 1) % nx, (x + 2) % nx

    def at_z(zz):
        return (zz * nyc + yc, x)

    def at_y(yy):
        return ((z * n + yy) * 2 + c, x)

    def at_yc(other):
        return (z * nyc + other, x)

    place = (y, z)
    ring = (at_y, at_z)
    first = (at_z, at_y)
    sibling = (me + 1 - 2 * c, x)

    barrier = pltpu.get_barrier_semaphore()

    def greet(dev):
        pl.semaphore_signal(barrier, 1, device_id=dev, device_id_type=MESH)

    for other in (xp, xm, xo):
        greet((me, other))
    greet(sibling)

    @pl.loop(1, n)
    def _(k):
        greet(at_z((z + k) % n))
        greet(at_y((y + k) % n))

    loads = [
        pltpu.make_async_copy(src, dst, lsem.at[k])
        for k, (src, dst) in enumerate(
            (
                (w_up_in, w_up),
                (w_down_in, w_down),
                (tok_in, tok),
                (ids_in, ids),
                (pool_in, pool),
                (bias_in, bias),
                (gain_in, gain),
                (lengths_in, lengths),
            )
        )
    ]
    for load in loads:
        load.start()
    for load in loads[:3]:
        load.wait()
    both = jnp.concatenate([w_up[...].astype(F32), w_down[...].astype(F32)], axis=0).astype(BF16)
    shard[0] = both[:, :hh]
    shard[1] = both[:, hh:]
    pl.semaphore_wait(barrier, 2 * (n - 1) + 4)

    def first_hop(h, k):
        mine = (z, y)[h]
        other = (mine + k) % n
        slot = G.at[c, 0, y, z] if h == 0 else G.at[c, 1, z, y]
        return remote(shard.at[h], slot, p1s.at[h, other], p1r.at[h, mine], first[h](other))

    @pl.loop(1, n)
    def _(k):
        first_hop(0, k).start()
        first_hop(1, k).start()

    t_send = [
        remote(tok, T.at[0], ts.at[0], tr.at[0], (me, xp)),
        remote(tok, T.at[1], ts.at[1], tr.at[1], (me, xm)),
        remote(tok, T.at[2], ts.at[2], tr.at[2], (me, xo)),
    ]
    for t in t_send:
        t.start()
    G[c, 0, y, z] = shard[0]
    G[c, 1, z, y] = shard[1]

    loads[3].wait()
    owner, place_in, label_col = slots(ids, n)
    slot = iota((total, rows), 0)
    target0 = ((owner % nyc) * n + owner // nyc) * 2 + place_in
    target1 = owner * 2 + place_in
    pick0 = jnp.where(slot == target0, 1.0, 0.0).astype(BF16)
    pick1 = jnp.where(slot == target1, 1.0, 0.0).astype(BF16)
    lab = jnp.broadcast_to(label_col + 1.0, (rows, LAB)).astype(BF16)
    SL[...] = mm(pick0, lab).astype(BF16).reshape(nyc, 2 * n, LAB)
    lab_y = exchange(SL, RL, yc, nyc, at_yc, yls, ylr)
    lab_z = exchange(TL, L.at[0], z, n, at_z, zls, zlr)

    @pl.loop(1, n)
    def _(k):
        for h in range(2):
            mine = (z, y)[h]
            other = (mine + k) % n
            slot_ = G.at[c, 0, y, other] if h == 0 else G.at[c, 1, z, other]
            remote(shard.at[h], slot_, p1s.at[h, other], p1r.at[h, other], first[h](other)).wait_recv()

    def second_hop(h, k):
        q = place[h]
        other = (q + k) % n
        return remote(G.at[c, h, q], G.at[c, h, q], ws.at[h, other], wr.at[h, q], ring[h](other))

    def to_sibling(h, i):
        return remote(G.at[c, h, i], G.at[c, h, i], sibs.at[h, i], sibr.at[h, i], sibling)

    @pl.loop(1, n)
    def _(k):
        second_hop(0, k).start()
        second_hop(1, k).start()

    lab_y[0]()
    to_sibling(0, y).start()
    to_sibling(1, z).start()

    for load in loads[4:]:
        load.wait()
    pool_n = pool.shape[0]
    emb[0:pool_n, :] = unit_rows(pool[...].astype(F32))

    row, col = iota((total, total), 0), iota((total, total), 1)
    z_, yc_, s_ = row // (2 * nyc), (row // 2) % nyc, row % 2
    by_z = jnp.where(col == (yc_ * n + z_) * 2 + s_, 1.0, 0.0).astype(BF16)
    yc_, z_ = row // (2 * n), (row // 2) % n
    by_yc = jnp.where(col == (z_ * nyc + yc_) * 2 + s_, 1.0, 0.0).astype(BF16)
    eye = row == col
    lab_y[1]()
    TL[...] = mm(by_z, RL[...].reshape(total, LAB)).astype(BF16).reshape(n, 2 * nyc, LAB)
    lab_z[0]()

    @pl.loop(1, n)
    def _(k):
        for h in range(2):
            other = (place[h] + k) % n
            g = G.at[c, h, other]
            remote(g, g, ws.at[h, other], wr.at[h, other], ring[h](other)).wait_recv()
            to_sibling(h, other).start()

    lab_z[1]()
    lx = [
        remote(L.at[0], L.at[1], lxs.at[0], lxr.at[0], (me, xp)),
        remote(L.at[0], L.at[2], lxs.at[1], lxr.at[1], (me, xm)),
    ]
    for t in lx:
        t.start()

    m = n * 16
    o, i_ = iota((2 * m, 2 * m), 0), iota((2 * m, 2 * m), 1)
    w_, rest = o // m, o % m
    n_, c_, r_ = rest // 16, (rest // 8) % 2, rest % 8
    order = jnp.where(i_ == c_ * m + n_ * 16 + w_ * 8 + r_, 1.0, 0.0).astype(BF16)

    @pl.loop(0, n)
    def _(i):
        for h in range(2):
            g = G.at[1 - c, h, i]
            remote(g, g, sibs.at[h, i], sibr.at[h, i], sibling).wait_recv()

    @pl.loop(0, n)
    def _(i):
        for h in range(2):
            pair = jnp.concatenate([G[0, h, i].reshape(m, hh), G[1, h, i].reshape(m, hh)], axis=0)
            w = mm(order, pair).astype(BF16)
            cols = slice(h * hh, (h + 1) * hh)
            for ref, part in ((up, w[:m]), (down, w[m:])):
                if h == 0:
                    for zz in range(n):
                        at = pl.multiple_of((zz * n + i) * 16, 16)
                        ref[pl.ds(at, 16), cols] = part[zz * 16 : (zz + 1) * 16]
                else:
                    ref[pl.ds(pl.multiple_of(i * m, m), m), cols] = part

    def ffn(block):
        pre = mm(block, up[...]) + bias[...].astype(F32).reshape(1, up.shape[1])
        hidden = (0.5 * pre * (1.0 + lax.erf(pre * (0.5**0.5)))).astype(BF16)
        return mm_nt(hidden, down[...])

    half = toks // 2
    lo, hi = pl.ds(0, half), pl.ds(half, half)
    sums = []

    def give(j, rows_, dst, to):
        k = len(sums)
        sums.append(remote(PS.at[j, rows_], dst, qs.at[k], qr.at[k], (me, to)))
        sums[-1].start()

    t_send[2].wait_recv()
    PS[2] = ffn(T[2]).astype(BF16)
    give(2, lo, RF.at[0], xp)
    give(2, hi, RF.at[1], xm)
    t_send[1].wait_recv()
    right = ffn(T[1])
    PS[1, hi] = right[half:].astype(BF16)
    give(1, hi, RA.at[0, hi], xp)
    t_send[0].wait_recv()
    left = ffn(T[0])
    PS[0, lo] = left[:half].astype(BF16)
    give(0, lo, RA.at[1, lo], xm)
    sums[0].wait_recv()
    PS[1, lo] = (right[:half] + RF[0].astype(F32)).astype(BF16)
    give(1, lo, RA.at[0, lo], xp)
    sums[1].wait_recv()
    PS[0, hi] = (left[half:] + RF[1].astype(F32)).astype(BF16)
    give(0, hi, RA.at[1, hi], xm)
    state = tok[...].astype(F32) + ffn(tok[...])
    for q in sums[2:]:
        q.wait_recv()
    state = state + RA[0].astype(F32) + RA[1].astype(F32)

    mean = jnp.mean(state, axis=1, keepdims=True)
    centred = state - mean
    var = jnp.mean(centred * centred, axis=1, keepdims=True)
    normed = centred * lax.rsqrt(var + 1e-05) * gain[...]
    docs = lengths.shape[1]
    len_row = lengths[...].astype(F32)
    len_col = to_column(len_row, docs)
    upto = iota((docs, docs), 1) <= iota((docs, docs), 0)
    ends = jnp.sum(jnp.where(upto, len_row, 0.0), axis=1, keepdims=True)
    places = iota((docs, toks), 1).astype(F32)
    member = jnp.where((places >= ends - len_col) & (places < ends), 1.0, 0.0)
    pooled = (
        jnp.dot(member, normed, precision=lax.Precision.HIGHEST, preferred_element_type=F32)
        / len_col
    )
    emb[pool_n : pool_n + docs, :] = unit_rows(pooled)

    w = d // 4
    p_y = [exchange(SP.at[k], RP.at[k], yc, nyc, at_yc, yps.at[k], ypr.at[k]) for k in range(2)]
    p_z = [exchange(TP.at[k], FP.at[k], z, n, at_z, zps.at[k], zpr.at[k]) for k in range(2)]
    q_z = [exchange(SQ.at[k], RQ.at[k], z, n, at_z, zqs.at[k], zqr.at[k]) for k in range(2)]
    q_y = [exchange(TQ.at[k], FQ.at[k], yc, nyc, at_yc, yqs.at[k], yqr.at[k]) for k in range(2)]
    for k in range(2):
        e0 = emb[:, 2 * k * w : (2 * k + 1) * w]
        e1 = emb[:, (2 * k + 1) * w : (2 * k + 2) * w]
        SP[k] = mm(pick0, e0).astype(BF16).reshape(nyc, 2 * n, w)
        p_y[k][0]()
        SQ[k] = mm(pick1, e1).astype(BF16).reshape(n, 2 * nyc, w)
        q_z[k][0]()
    for k in range(2):
        p_y[k][1]()
        TP[k] = mm(by_z, RP[k].reshape(total, w)).astype(BF16).reshape(n, 2 * nyc, w)
        p_z[k][0]()
        q_z[k][1]()
        TQ[k] = mm(by_yc, RQ[k].reshape(total, w)).astype(BF16).reshape(nyc, 2 * n, w)
        q_y[k][0]()

    xs = []
    for k in range(2):
        p_z[k][1]()
        E[0, k, :, :w] = FP[k].reshape(total, w)
        q_y[k][1]()
        E[0, k, :, w:] = mm(by_z, FQ[k].reshape(total, w)).astype(BF16)
        xs.append(remote(E.at[0, k], E.at[1, k], es.at[0, k], er.at[0, k], (me, xp)))
        xs.append(remote(E.at[0, k], E.at[2, k], es.at[1, k], er.at[1, k], (me, xm)))
        xs[-2].start()
        xs[-1].start()

    for t in lx:
        t.wait_recv()

    def labels(i):
        column = L[i].reshape(total, LAB)[:, 0:1].astype(F32)
        return column, jnp.sum(jnp.where(eye, column, 0.0), axis=0, keepdims=True)

    (col0, row0), (col1, row1), (col2, _) = labels(0), labels(1), labels(2)

    def part(j, i, k):
        return mm_nt(E[j, k], E[i, k])

    def best_of(sc, keep):
        return jnp.max(jnp.where(keep, sc, -1.0), axis=0, keepdims=True)

    best = best_of(part(0, 0, 0) + part(0, 0, 1), (col0 == row0) & ~eye)
    xs[0].wait_recv()
    xs[1].wait_recv()
    s21, s10, s20 = part(2, 1, 0), part(1, 0, 0), part(2, 0, 0)
    xs[2].wait_recv()
    xs[3].wait_recv()
    B1[1] = jnp.broadcast_to(best_of(s21 + part(2, 1, 1), col2 == row1), B1.shape[1:])
    over = B1.at[1, pl.ds(0, 1)]

    @pl.loop(0, n)
    def _(zz):
        remote(over, BM.at[z], bms.at[zz], bmr.at[z], (zz * nyc + yc, xm)).start()

    best = jnp.maximum(best, best_of(s10 + part(1, 0, 1), col1 == row0))
    best = jnp.maximum(best, best_of(s20 + part(2, 0, 1), col2 == row0))
    B1[0] = jnp.broadcast_to(best, B1.shape[1:])

    back_z = exchange(B1.at[0, pl.ds(0, 1)], B2, z, n, at_z, b1s, b1r, spread=True)
    back_z[0]()

    @pl.loop(0, n)
    def _(zz):
        remote(over, BM.at[zz], bms.at[zz], bmr.at[zz], (zz * nyc + yc, xm)).wait()

    back_z[1]()
    both_ = jnp.maximum(B2[...], BM[...]).reshape(n, total)
    LR[...] = pltpu.roll(both_, (total - z * 2 * nyc) % total, 1)[:, : LR.shape[1]]
    back_y = exchange(LR, B3, yc, nyc, at_yc, b2s, b2r, spread=True)
    back_y[0]()
    back_y[1]()
    got = B3[...].reshape(dp, LR.shape[1])
    lane = iota(got.shape, 1)
    v0 = jnp.sum(jnp.where(lane == yc * 2, got, 0.0), axis=1, keepdims=True)
    v1 = jnp.sum(jnp.where(lane == yc * 2 + 1, got, 0.0), axis=1, keepdims=True)
    mine = iota((dp, rows), 0) == (owner % nyc) * n + owner // nyc
    out[...] = jnp.sum(jnp.where(mine, jnp.where(place_in == 0, v0, v1), 0.0), axis=0, keepdims=True)

    @pl.loop(1, n)
    def _(k):
        for h in range(2):
            first_hop(h, k).wait_send()
            second_hop(h, k).wait_send()

    @pl.loop(0, n)
    def _(i):
        to_sibling(0, i).wait_send()
        to_sibling(1, i).wait_send()

    for t in [*t_send, *sums, *lx, *xs]:
        t.wait_send()


ANY = pl.BlockSpec(memory_space=pl.ANY)


def on_device(n, nx, tokens, w_up, b_up, w_down, ln_gain, doc_lengths, pool_rows, cluster_ids):
    toks, d = tokens.shape
    hid = w_up.shape[1]
    hh = hid // 2
    rows = cluster_ids.shape[0]
    nyc = 2 * n
    dp = nyc * n
    total = 2 * dp
    w = d // 4
    keep = min(total, 128)

    def vm(*shape):
        return pltpu.VMEM(shape, BF16)

    def vf(*shape):
        return pltpu.VMEM(shape, F32)

    def two(*shape):
        return [pltpu.SemaphoreType.DMA(shape)] * 2

    out = pl.pallas_call(
        functools.partial(kernel, n, nx),
        out_shape=jax.ShapeDtypeStruct((1, rows), F32),
        in_specs=[ANY] * 8,
        out_specs=pl.BlockSpec(memory_space=pltpu.VMEM),
        scratch_shapes=[
            vm(toks, d),
            vm(*w_up.shape),
            vm(*w_up.shape),
            vm(hid),
            vf(1, d),
            pltpu.VMEM(doc_lengths.shape, jnp.int32),
            vm(*pool_rows.shape),
            pltpu.VMEM((1, rows), jnp.int32),
            vm(2, 16, hh),
            vm(2, 2, n, n, 16, hh),
            vm(3, toks, d),
            vm(d, hid),
            vm(d, hid),
            vm(3, toks, d),
            vm(2, toks, d),
            vm(2, toks // 2, d),
            vm(rows, d),
            vm(nyc, 2 * n, LAB),
            vm(nyc, 2 * n, LAB),
            vm(n, 2 * nyc, LAB),
            vm(3, n, 2 * nyc, LAB),
            vm(2, nyc, 2 * n, w),
            vm(2, nyc, 2 * n, w),
            vm(2, n, 2 * nyc, w),
            vm(2, n, 2 * nyc, w),
            vm(2, n, 2 * nyc, w),
            vm(2, n, 2 * nyc, w),
            vm(2, nyc, 2 * n, w),
            vm(2, nyc, 2 * n, w),
            vm(3, 2, total, 2 * w),
            vf(2, 8, total),
            vf(n, 1, total),
            vf(n, 1, total),
            vf(n, keep),
            vf(nyc, n, keep),
            pltpu.SemaphoreType.DMA((8,)),
            *two(2, n),
            *two(2, n),
            *two(2, n),
            *two(3),
            *two(6),
            *two(nyc),
            *two(n),
            *two(2),
            *two(2, nyc),
            *two(2, n),
            *two(2, n),
            *two(2, nyc),
            *two(2, 2),
            *two(n),
            *two(n),
            *two(nyc),
        ],
        compiler_params=pltpu.CompilerParams(
            collective_id=0, has_side_effects=True, vmem_limit_bytes=58 * 2**20
        ),
    )(
        tokens,
        w_up,
        w_down.T,
        b_up,
        ln_gain.reshape(1, d),
        doc_lengths,
        pool_rows,
        cluster_ids.reshape(1, rows),
    )
    return out.reshape(rows)


def solution(mesh):
    n = math.isqrt(mesh.shape["dp"] // 2)
    placed = (
        P(("dp", "split"), None),
        P("dp", "split"),
        P("split"),
        P("split", "dp"),
        P(),
        P(("dp", "split"), None),
        P(("dp", "split"), None),
        P(("dp", "split")),
    )
    return jax.shard_map(
        functools.partial(on_device, n, mesh.shape["split"]),
        mesh=mesh,
        in_specs=placed,
        out_specs=P(("dp", "split")),
        check_vma=False,
    )
```

```python
import functools
import math

import jax
import jax.numpy as jnp
from jax import lax
from jax.experimental import pallas as pl
from jax.experimental.pallas import tpu as pltpu
from jax.sharding import PartitionSpec as P

MESH = pl.DeviceIdType.MESH
F32, BF16 = jnp.float32, jnp.bfloat16
LAB = 128


def iota(shape, dim):
    return lax.broadcasted_iota(jnp.int32, shape, dim)


def div(a, k):
    return a >> (k.bit_length() - 1)


def mod(a, k):
    return a & (k - 1)


def mm(a, b):
    return jnp.dot(a, b, preferred_element_type=F32)


def mm_nt(a, b):
    return lax.dot_general(a, b, (((1,), (1,)), ((), ())), preferred_element_type=F32)


def unit_rows(v):
    return (v * lax.rsqrt(jnp.sum(v * v, axis=1, keepdims=True) + 1e-06)).astype(BF16)


def here(n):
    me = lax.axis_index("dp")
    return me, me // (2 * n), (me // 2) % n, me % 2, lax.axis_index("split")


def to_column(row, size):
    eye = iota((size, size), 0) == iota((size, size), 1)
    return jnp.sum(jnp.where(eye, row, 0.0), axis=1, keepdims=True)


def slots(ids_ref, n):
    dp = 2 * n * n
    rows = ids_ref.shape[1]
    ids = ids_ref[...]
    owner, label = mod(ids, dp), div(ids, dp)
    owner_col = to_column(owner.astype(F32), rows)
    same = owner_col == owner.astype(F32)
    before = iota((rows, rows), 0) < iota((rows, rows), 1)
    place = jnp.sum(jnp.where(same & before, 1.0, 0.0), axis=0, keepdims=True).astype(jnp.int32)
    return owner, place, to_column(label.astype(F32), rows)


def remote(src, dst, send, recv, dev):
    return pltpu.make_async_remote_copy(
        src_ref=src, dst_ref=dst, send_sem=send, recv_sem=recv, device_id=dev, device_id_type=MESH
    )


def exchange(src, dst, mine, count, dev, send, recv, spread=False):
    def piece(other):
        return src if spread else src.at[other]

    def start():
        @pl.loop(1, count)
        def _(k):
            other = (mine + k) % count
            remote(piece(other), dst.at[mine], send.at[other], recv.at[mine], dev(other)).start()

        dst[mine] = src[...] if spread else src[mine]

    def wait():
        @pl.loop(1, count)
        def _(k):
            other = (mine + k) % count
            remote(piece(other), dst.at[other], send.at[other], recv.at[other], dev(other)).wait()

    return start, wait


def kernel(
    n, nx, tok_in, w_up_in, w_down_in, bias_in, gain_in, lengths_in, pool_in, ids_in, out,
    tok, w_up, w_down, bias, gain, lengths, pool, ids, shard, G, T, up, down, PS, RA, RF, emb,
    SL, RL, TL, L, SP, RP, TP, FP, SQ, RQ, TQ, FQ, E, B1, B2, BM, LR, B3,
    lsem, p1s, p1r, ws, wr, sibs, sibr, ts, tr, qs, qr,
    yls, ylr, zls, zlr, lxs, lxr, yps, ypr, zps, zpr, zqs, zqr, yqs, yqr, es, er,
    b1s, b1r, bms, bmr, b2s, b2r,
):
    me, z, y, c, x = here(n)
    nyc = 2 * n
    yc = me % nyc
    dp = nyc * n
    total = 2 * dp
    hh = shard.shape[2]
    toks, d = tok.shape
    rows = ids.shape[1]
    xp, xm, xo = (x + 1) % nx, (x + nx - 1) % nx, (x + 2) % nx

    def at_z(zz):
        return (zz * nyc + yc, x)

    def at_y(yy):
        return ((z * n + yy) * 2 + c, x)

    def at_yc(other):
        return (z * nyc + other, x)

    place = (y, z)
    ring = (at_y, at_z)
    first = (at_z, at_y)
    sibling = (me + 1 - 2 * c, x)

    barrier = pltpu.get_barrier_semaphore()

    def greet(dev):
        pl.semaphore_signal(barrier, 1, device_id=dev, device_id_type=MESH)

    for other in (xp, xm, xo):
        greet((me, other))
    greet(sibling)

    @pl.loop(1, n)
    def _(k):
        greet(at_z((z + k) % n))
        greet(at_y((y + k) % n))

    loads = [
        pltpu.make_async_copy(src, dst, lsem.at[k])
        for k, (src, dst) in enumerate(
            (
                (w_up_in, w_up),
                (w_down_in, w_down),
                (tok_in, tok),
                (ids_in, ids),
                (pool_in, pool),
                (bias_in, bias),
                (gain_in, gain),
                (lengths_in, lengths),
            )
        )
    ]
    for load in loads:
        load.start()
    for load in loads[:3]:
        load.wait()
    both = jnp.concatenate([w_up[...].astype(F32), w_down[...].astype(F32)], axis=0).astype(BF16)
    shard[0] = both[:, :hh]
    shard[1] = both[:, hh:]
    pl.semaphore_wait(barrier, 2 * (n - 1) + 4)

    def first_hop(h, k):
        mine = (z, y)[h]
        other = (mine + k) % n
        slot = G.at[c, 0, y, z] if h == 0 else G.at[c, 1, z, y]
        return remote(shard.at[h], slot, p1s.at[h, other], p1r.at[h, mine], first[h](other))

    @pl.loop(1, n)
    def _(k):
        first_hop(0, k).start()
        first_hop(1, k).start()

    t_send = [
        remote(tok, T.at[0], ts.at[0], tr.at[0], (me, xp)),
        remote(tok, T.at[1], ts.at[1], tr.at[1], (me, xm)),
        remote(tok, T.at[2], ts.at[2], tr.at[2], (me, xo)),
    ]
    for t in t_send:
        t.start()
    G[c, 0, y, z] = shard[0]
    G[c, 1, z, y] = shard[1]

    loads[3].wait()
    owner, place_in, label_col = slots(ids, n)
    slot = iota((total, rows), 0)
    owner_at = mod(owner, nyc) * n + div(owner, nyc)
    target0 = owner_at * 2 + place_in
    target1 = owner * 2 + place_in
    pick0 = jnp.where(slot == target0, 1.0, 0.0).astype(BF16)
    pick1 = jnp.where(slot == target1, 1.0, 0.0).astype(BF16)
    lab = jnp.broadcast_to(label_col + 1.0, (rows, LAB)).astype(BF16)
    SL[...] = mm(pick0, lab).astype(BF16).reshape(nyc, 2 * n, LAB)
    lab_y = exchange(SL, RL, yc, nyc, at_yc, yls, ylr)
    lab_z = exchange(TL, L.at[0], z, n, at_z, zls, zlr)

    row, col = iota((total, total), 0), iota((total, total), 1)
    eye = row == col
    s_ = mod(row, 2)
    from_ = (mod(div(row, 2), nyc) * n + div(row, 2 * nyc)) * 2 + s_
    by_z = jnp.where(col == from_, 1.0, 0.0).astype(BF16)
    from_ = (mod(div(row, 2), n) * nyc + div(row, 2 * n)) * 2 + s_
    by_yc = jnp.where(col == from_, 1.0, 0.0).astype(BF16)

    m = n * 16
    o, i_ = iota((2 * m, 2 * m), 0), iota((2 * m, 2 * m), 1)
    rest = mod(o, m)
    from_ = mod(div(rest, 8), 2) * m + div(rest, 16) * 16 + div(o, m) * 8 + mod(rest, 8)
    order = jnp.where(i_ == from_, 1.0, 0.0).astype(BF16)

    @pl.loop(1, n)
    def _(k):
        for h in range(2):
            mine = (z, y)[h]
            other = (mine + k) % n
            slot_ = G.at[c, 0, y, other] if h == 0 else G.at[c, 1, z, other]
            remote(shard.at[h], slot_, p1s.at[h, other], p1r.at[h, other], first[h](other)).wait_recv()

    def second_hop(h, k):
        q = place[h]
        other = (q + k) % n
        return remote(G.at[c, h, q], G.at[c, h, q], ws.at[h, other], wr.at[h, q], ring[h](other))

    def to_sibling(h, i):
        return remote(G.at[c, h, i], G.at[c, h, i], sibs.at[h, i], sibr.at[h, i], sibling)

    @pl.loop(1, n)
    def _(k):
        second_hop(0, k).start()
        second_hop(1, k).start()

    lab_y[0]()
    to_sibling(0, y).start()
    to_sibling(1, z).start()

    for load in loads[4:]:
        load.wait()
    pool_n = pool.shape[0]
    emb[0:pool_n, :] = unit_rows(pool[...].astype(F32))


    def pass_on(h, other):
        g = G.at[c, h, other]
        remote(g, g, ws.at[h, other], wr.at[h, other], ring[h](other)).wait_recv()
        to_sibling(h, other).start()

    @pl.loop(1, n // 2)
    def _(k):
        for h in range(2):
            pass_on(h, (place[h] + k) % n)
            pass_on(h, (place[h] + n - k) % n)

    for h in range(2):
        pass_on(h, (place[h] + n // 2) % n)

    @pl.loop(0, n)
    def _(i):
        for h in range(2):
            g = G.at[1 - c, h, i]
            remote(g, g, sibs.at[h, i], sibr.at[h, i], sibling).wait_recv()

    @pl.loop(0, n)
    def _(i):
        for h in range(2):
            pair = jnp.concatenate([G[0, h, i].reshape(m, hh), G[1, h, i].reshape(m, hh)], axis=0)
            w = mm(order, pair).astype(BF16)
            cols = slice(h * hh, (h + 1) * hh)
            for ref, part in ((up, w[:m]), (down, w[m:])):
                if h == 0:
                    for zz in range(n):
                        at = pl.multiple_of((zz * n + i) * 16, 16)
                        ref[pl.ds(at, 16), cols] = part[zz * 16 : (zz + 1) * 16]
                else:
                    ref[pl.ds(pl.multiple_of(i * m, m), m), cols] = part

    def ffn(block):
        pre = mm(block, up[...]) + bias[...].astype(F32).reshape(1, up.shape[1])
        hidden = (0.5 * pre * (1.0 + lax.erf(pre * (0.5**0.5)))).astype(BF16)
        return mm_nt(hidden, down[...])

    half = toks // 2
    lo, hi = pl.ds(0, half), pl.ds(half, half)
    sums = []

    def give(j, rows_, dst, to):
        k = len(sums)
        sums.append(remote(PS.at[j, rows_], dst, qs.at[k], qr.at[k], (me, to)))
        sums[-1].start()

    t_send[2].wait_recv()
    PS[2] = ffn(T[2]).astype(BF16)
    give(2, lo, RF.at[0], xp)
    give(2, hi, RF.at[1], xm)
    t_send[1].wait_recv()
    right = ffn(T[1])
    PS[1, hi] = right[half:].astype(BF16)
    give(1, hi, RA.at[0, hi], xp)
    t_send[0].wait_recv()
    left = ffn(T[0])
    PS[0, lo] = left[:half].astype(BF16)
    give(0, lo, RA.at[1, lo], xm)
    lab_y[1]()
    TL[...] = mm(by_z, RL[...].reshape(total, LAB)).astype(BF16).reshape(n, 2 * nyc, LAB)
    lab_z[0]()

    sums[0].wait_recv()
    PS[1, lo] = (right[:half] + RF[0].astype(F32)).astype(BF16)
    give(1, lo, RA.at[0, lo], xp)
    sums[1].wait_recv()
    PS[0, hi] = (left[half:] + RF[1].astype(F32)).astype(BF16)
    give(0, hi, RA.at[1, hi], xm)
    state = tok[...].astype(F32) + ffn(tok[...])
    for q in sums[2:]:
        q.wait_recv()
    state = state + RA[0].astype(F32) + RA[1].astype(F32)

    mean = jnp.mean(state, axis=1, keepdims=True)
    centred = state - mean
    var = jnp.mean(centred * centred, axis=1, keepdims=True)
    normed = centred * lax.rsqrt(var + 1e-05) * gain[...]
    docs = lengths.shape[1]
    len_row = lengths[...].astype(F32)
    len_col = to_column(len_row, docs)
    upto = iota((docs, docs), 1) <= iota((docs, docs), 0)
    ends = jnp.sum(jnp.where(upto, len_row, 0.0), axis=1, keepdims=True)
    places = iota((docs, toks), 1).astype(F32)
    member = jnp.where((places >= ends - len_col) & (places < ends), 1.0, 0.0)
    pooled = (
        jnp.dot(member, normed, precision=lax.Precision.HIGHEST, preferred_element_type=F32)
        / len_col
    )
    emb[pool_n : pool_n + docs, :] = unit_rows(pooled)

    w = d // 4
    p_y = [exchange(SP.at[k], RP.at[k], yc, nyc, at_yc, yps.at[k], ypr.at[k]) for k in range(2)]
    p_z = [exchange(TP.at[k], FP.at[k], z, n, at_z, zps.at[k], zpr.at[k]) for k in range(2)]
    q_z = [exchange(SQ.at[k], RQ.at[k], z, n, at_z, zqs.at[k], zqr.at[k]) for k in range(2)]
    q_y = [exchange(TQ.at[k], FQ.at[k], yc, nyc, at_yc, yqs.at[k], yqr.at[k]) for k in range(2)]
    for k in range(2):
        e0 = emb[:, 2 * k * w : (2 * k + 1) * w]
        e1 = emb[:, (2 * k + 1) * w : (2 * k + 2) * w]
        SP[k] = mm(pick0, e0).astype(BF16).reshape(nyc, 2 * n, w)
        p_y[k][0]()
        SQ[k] = mm(pick1, e1).astype(BF16).reshape(n, 2 * nyc, w)
        q_z[k][0]()
    lab_z[1]()
    lx = [
        remote(L.at[0], L.at[1], lxs.at[0], lxr.at[0], (me, xp)),
        remote(L.at[0], L.at[2], lxs.at[1], lxr.at[1], (me, xm)),
    ]
    for t in lx:
        t.start()
    for k in range(2):
        p_y[k][1]()
        TP[k] = mm(by_z, RP[k].reshape(total, w)).astype(BF16).reshape(n, 2 * nyc, w)
        p_z[k][0]()
        q_z[k][1]()
        TQ[k] = mm(by_yc, RQ[k].reshape(total, w)).astype(BF16).reshape(nyc, 2 * n, w)
        q_y[k][0]()

    xs = []
    for k in range(2):
        p_z[k][1]()
        E[0, k, :, :w] = FP[k].reshape(total, w)
        q_y[k][1]()
        E[0, k, :, w:] = mm(by_z, FQ[k].reshape(total, w)).astype(BF16)
        xs.append(remote(E.at[0, k], E.at[1, k], es.at[0, k], er.at[0, k], (me, xp)))
        xs.append(remote(E.at[0, k], E.at[2, k], es.at[1, k], er.at[1, k], (me, xm)))
        xs[-2].start()
        xs[-1].start()

    for t in lx:
        t.wait_recv()

    def labels(i):
        column = L[i].reshape(total, LAB)[:, 0:1].astype(F32)
        return column, jnp.sum(jnp.where(eye, column, 0.0), axis=0, keepdims=True)

    (col0, row0), (col1, row1), (col2, _) = labels(0), labels(1), labels(2)

    def part(j, i, k):
        return mm_nt(E[j, k], E[i, k])

    def best_of(sc, keep):
        return jnp.max(jnp.where(keep, sc, -1.0), axis=0, keepdims=True)

    best = best_of(part(0, 0, 0) + part(0, 0, 1), (col0 == row0) & ~eye)
    xs[0].wait_recv()
    xs[1].wait_recv()
    s21, s10, s20 = part(2, 1, 0), part(1, 0, 0), part(2, 0, 0)
    xs[2].wait_recv()
    xs[3].wait_recv()
    B1[1] = jnp.broadcast_to(best_of(s21 + part(2, 1, 1), col2 == row1), B1.shape[1:])
    over = B1.at[1, pl.ds(0, 1)]

    @pl.loop(0, n)
    def _(zz):
        remote(over, BM.at[z], bms.at[zz], bmr.at[z], (zz * nyc + yc, xm)).start()

    best = jnp.maximum(best, best_of(s10 + part(1, 0, 1), col1 == row0))
    best = jnp.maximum(best, best_of(s20 + part(2, 0, 1), col2 == row0))
    B1[0] = jnp.broadcast_to(best, B1.shape[1:])

    back_z = exchange(B1.at[0, pl.ds(0, 1)], B2, z, n, at_z, b1s, b1r, spread=True)
    back_z[0]()

    @pl.loop(0, n)
    def _(zz):
        remote(over, BM.at[zz], bms.at[zz], bmr.at[zz], (zz * nyc + yc, xm)).wait()

    back_z[1]()
    both_ = jnp.maximum(B2[...], BM[...]).reshape(n, total)
    LR[...] = pltpu.roll(both_, (total - z * 2 * nyc) % total, 1)[:, : LR.shape[1]]
    back_y = exchange(LR, B3, yc, nyc, at_yc, b2s, b2r, spread=True)
    back_y[0]()
    back_y[1]()
    got = B3[...].reshape(dp, LR.shape[1])
    lane = iota(got.shape, 1)
    v0 = jnp.sum(jnp.where(lane == yc * 2, got, 0.0), axis=1, keepdims=True)
    v1 = jnp.sum(jnp.where(lane == yc * 2 + 1, got, 0.0), axis=1, keepdims=True)
    mine = iota((dp, rows), 0) == owner_at
    out[...] = jnp.sum(jnp.where(mine, jnp.where(place_in == 0, v0, v1), 0.0), axis=0, keepdims=True)

    @pl.loop(1, n)
    def _(k):
        for h in range(2):
            first_hop(h, k).wait_send()
            second_hop(h, k).wait_send()

    @pl.loop(0, n)
    def _(i):
        to_sibling(0, i).wait_send()
        to_sibling(1, i).wait_send()

    for t in [*t_send, *sums, *lx, *xs]:
        t.wait_send()


ANY = pl.BlockSpec(memory_space=pl.ANY)


def on_device(n, nx, tokens, w_up, b_up, w_down, ln_gain, doc_lengths, pool_rows, cluster_ids):
    toks, d = tokens.shape
    hid = w_up.shape[1]
    hh = hid // 2
    rows = cluster_ids.shape[0]
    nyc = 2 * n
    dp = nyc * n
    total = 2 * dp
    w = d // 4
    keep = min(total, 128)

    def vm(*shape):
        return pltpu.VMEM(shape, BF16)

    def vf(*shape):
        return pltpu.VMEM(shape, F32)

    def two(*shape):
        return [pltpu.SemaphoreType.DMA(shape)] * 2

    out = pl.pallas_call(
        functools.partial(kernel, n, nx),
        out_shape=jax.ShapeDtypeStruct((1, rows), F32),
        in_specs=[ANY] * 8,
        out_specs=pl.BlockSpec(memory_space=pltpu.VMEM),
        scratch_shapes=[
            vm(toks, d),
            vm(*w_up.shape),
            vm(*w_up.shape),
            vm(hid),
            vf(1, d),
            pltpu.VMEM(doc_lengths.shape, jnp.int32),
            vm(*pool_rows.shape),
            pltpu.VMEM((1, rows), jnp.int32),
            vm(2, 16, hh),
            vm(2, 2, n, n, 16, hh),
            vm(3, toks, d),
            vm(d, hid),
            vm(d, hid),
            vm(3, toks, d),
            vm(2, toks, d),
            vm(2, toks // 2, d),
            vm(rows, d),
            vm(nyc, 2 * n, LAB),
            vm(nyc, 2 * n, LAB),
            vm(n, 2 * nyc, LAB),
            vm(3, n, 2 * nyc, LAB),
            vm(2, nyc, 2 * n, w),
            vm(2, nyc, 2 * n, w),
            vm(2, n, 2 * nyc, w),
            vm(2, n, 2 * nyc, w),
            vm(2, n, 2 * nyc, w),
            vm(2, n, 2 * nyc, w),
            vm(2, nyc, 2 * n, w),
            vm(2, nyc, 2 * n, w),
            vm(3, 2, total, 2 * w),
            vf(2, 8, total),
            vf(n, 1, total),
            vf(n, 1, total),
            vf(n, keep),
            vf(nyc, n, keep),
            pltpu.SemaphoreType.DMA((8,)),
            *two(2, n),
            *two(2, n),
            *two(2, n),
            *two(3),
            *two(6),
            *two(nyc),
            *two(n),
            *two(2),
            *two(2, nyc),
            *two(2, n),
            *two(2, n),
            *two(2, nyc),
            *two(2, 2),
            *two(n),
            *two(n),
            *two(nyc),
        ],
        compiler_params=pltpu.CompilerParams(
            collective_id=0, has_side_effects=True, vmem_limit_bytes=58 * 2**20
        ),
    )(
        tokens,
        w_up,
        w_down.T,
        b_up,
        ln_gain.reshape(1, d),
        doc_lengths,
        pool_rows,
        cluster_ids.reshape(1, rows),
    )
    return out.reshape(rows)


def solution(mesh):
    n = math.isqrt(mesh.shape["dp"] // 2)
    placed = (
        P(("dp", "split"), None),
        P("dp", "split"),
        P("split"),
        P("split", "dp"),
        P(),
        P(("dp", "split"), None),
        P(("dp", "split"), None),
        P(("dp", "split")),
    )
    return jax.shard_map(
        functools.partial(on_device, n, mesh.shape["split"]),
        mesh=mesh,
        in_specs=placed,
        out_specs=P(("dp", "split")),
        check_vma=False,
    )
```

```python
import functools
import math

import jax
import jax.numpy as jnp
from jax import lax
from jax.experimental import pallas as pl
from jax.experimental.pallas import tpu as pltpu
from jax.sharding import PartitionSpec as P

MESH = pl.DeviceIdType.MESH
F32, BF16 = jnp.float32, jnp.bfloat16
LAB = 128


def iota(shape, dim):
    return lax.broadcasted_iota(jnp.int32, shape, dim)


def div(a, k):
    return a >> (k.bit_length() - 1)


def mod(a, k):
    return a & (k - 1)


def mm(a, b):
    return jnp.dot(a, b, preferred_element_type=F32)


def mm_nt(a, b):
    return lax.dot_general(a, b, (((1,), (1,)), ((), ())), preferred_element_type=F32)


def unit_rows(v):
    return (v * lax.rsqrt(jnp.sum(v * v, axis=1, keepdims=True) + 1e-06)).astype(BF16)


def here(n):
    me = lax.axis_index("dp")
    return me, me // (2 * n), (me // 2) % n, me % 2, lax.axis_index("split")


def to_column(row, size):
    eye = iota((size, size), 0) == iota((size, size), 1)
    return jnp.sum(jnp.where(eye, row, 0.0), axis=1, keepdims=True)


def slots(ids_ref, n):
    dp = 2 * n * n
    rows = ids_ref.shape[1]
    ids = ids_ref[...]
    owner, label = mod(ids, dp), div(ids, dp)
    owner_col = to_column(owner.astype(F32), rows)
    same = owner_col == owner.astype(F32)
    before = iota((rows, rows), 0) < iota((rows, rows), 1)
    place = jnp.sum(jnp.where(same & before, 1.0, 0.0), axis=0, keepdims=True).astype(jnp.int32)
    return owner, place, to_column(label.astype(F32), rows)


def remote(src, dst, send, recv, dev):
    return pltpu.make_async_remote_copy(
        src_ref=src, dst_ref=dst, send_sem=send, recv_sem=recv, device_id=dev, device_id_type=MESH
    )


def exchange(src, dst, mine, count, dev, send, recv, spread=False):
    def piece(other):
        return src if spread else src.at[other]

    def start():
        @pl.loop(1, count)
        def _(k):
            other = (mine + k) % count
            remote(piece(other), dst.at[mine], send.at[other], recv.at[mine], dev(other)).start()

        dst[mine] = src[...] if spread else src[mine]

    def wait():
        @pl.loop(1, count)
        def _(k):
            other = (mine + k) % count
            remote(piece(other), dst.at[other], send.at[other], recv.at[other], dev(other)).wait()

    return start, wait


def kernel(
    n, nx, tok_in, w_up_in, w_down_in, bias_in, gain_in, lengths_in, pool_in, ids_in, out,
    tok, w_up, w_down, bias, gain, lengths, pool, ids, shard, G, T, up, down, PS, RA, RF, emb,
    SL, RL, TL, L, SP, RP, TP, FP, SQ, RQ, TQ, FQ, E, B1, B2, BM, LR, B3,
    lsem, p1s, p1r, ws, wr, sibs, sibr, ts, tr, qs, qr,
    yls, ylr, zls, zlr, lxs, lxr, yps, ypr, zps, zpr, zqs, zqr, yqs, yqr, es, er,
    b1s, b1r, bms, bmr, b2s, b2r,
):
    me, z, y, c, x = here(n)
    nyc = 2 * n
    yc = me % nyc
    dp = nyc * n
    total = 2 * dp
    hh = shard.shape[2]
    toks, d = tok.shape
    rows = ids.shape[1]
    xp, xm, xo = (x + 1) % nx, (x + nx - 1) % nx, (x + 2) % nx

    def at_z(zz):
        return (zz * nyc + yc, x)

    def at_y(yy):
        return ((z * n + yy) * 2 + c, x)

    def at_yc(other):
        return (z * nyc + other, x)

    place = (y, z)
    ring = (at_y, at_z)
    first = (at_z, at_y)
    sibling = (me + 1 - 2 * c, x)

    barrier = pltpu.get_barrier_semaphore()

    def greet(dev):
        pl.semaphore_signal(barrier, 1, device_id=dev, device_id_type=MESH)

    for other in (xp, xm, xo):
        greet((me, other))
    greet(sibling)

    @pl.loop(1, n)
    def _(k):
        greet(at_z((z + k) % n))
        greet(at_y((y + k) % n))

    loads = [
        pltpu.make_async_copy(src, dst, lsem.at[k])
        for k, (src, dst) in enumerate(
            (
                (w_up_in, w_up),
                (w_down_in, w_down),
                (tok_in, tok),
                (ids_in, ids),
                (pool_in, pool),
                (bias_in, bias),
                (gain_in, gain),
                (lengths_in, lengths),
            )
        )
    ]
    for load in loads:
        load.start()
    for load in loads[:3]:
        load.wait()
    both = jnp.concatenate([w_up[...].astype(F32), w_down[...].astype(F32)], axis=0).astype(BF16)
    shard[0] = both[:, :hh]
    shard[1] = both[:, hh:]
    pl.semaphore_wait(barrier, 2 * (n - 1) + 4)

    def first_hop(h, k):
        mine = (z, y)[h]
        other = (mine + k) % n
        slot = G.at[c, 0, y, z] if h == 0 else G.at[c, 1, z, y]
        return remote(shard.at[h], slot, p1s.at[h, other], p1r.at[h, mine], first[h](other))

    @pl.loop(1, n)
    def _(k):
        first_hop(0, k).start()
        first_hop(1, k).start()

    t_send = [
        remote(tok, T.at[0], ts.at[0], tr.at[0], (me, xp)),
        remote(tok, T.at[1], ts.at[1], tr.at[1], (me, xm)),
        remote(tok, T.at[2], ts.at[2], tr.at[2], (me, xo)),
    ]
    for t in t_send:
        t.start()
    G[c, 0, y, z] = shard[0]
    G[c, 1, z, y] = shard[1]

    @pl.loop(1, n)
    def _(k):
        for h in range(2):
            mine = (z, y)[h]
            other = (mine + k) % n
            slot_ = G.at[c, 0, y, other] if h == 0 else G.at[c, 1, z, other]
            remote(shard.at[h], slot_, p1s.at[h, other], p1r.at[h, other], first[h](other)).wait_recv()

    def second_hop(h, k):
        q = place[h]
        other = (q + k) % n
        return remote(G.at[c, h, q], G.at[c, h, q], ws.at[h, other], wr.at[h, q], ring[h](other))

    def to_sibling(h, i):
        return remote(G.at[c, h, i], G.at[c, h, i], sibs.at[h, i], sibr.at[h, i], sibling)

    @pl.loop(1, n)
    def _(k):
        second_hop(0, k).start()
        second_hop(1, k).start()

    to_sibling(0, y).start()
    to_sibling(1, z).start()

    loads[3].wait()
    owner, place_in, label_col = slots(ids, n)
    slot = iota((total, rows), 0)
    owner_at = mod(owner, nyc) * n + div(owner, nyc)
    target0 = owner_at * 2 + place_in
    target1 = owner * 2 + place_in
    pick0 = jnp.where(slot == target0, 1.0, 0.0).astype(BF16)
    pick1 = jnp.where(slot == target1, 1.0, 0.0).astype(BF16)
    lab = jnp.broadcast_to(label_col + 1.0, (rows, LAB)).astype(BF16)
    SL[...] = mm(pick0, lab).astype(BF16).reshape(nyc, 2 * n, LAB)
    lab_y = exchange(SL, RL, yc, nyc, at_yc, yls, ylr)
    lab_z = exchange(TL, L.at[0], z, n, at_z, zls, zlr)

    row, col = iota((total, total), 0), iota((total, total), 1)
    eye = row == col
    s_ = mod(row, 2)
    from_ = (mod(div(row, 2), nyc) * n + div(row, 2 * nyc)) * 2 + s_
    by_z = jnp.where(col == from_, 1.0, 0.0).astype(BF16)
    from_ = (mod(div(row, 2), n) * nyc + div(row, 2 * n)) * 2 + s_
    by_yc = jnp.where(col == from_, 1.0, 0.0).astype(BF16)

    m = n * 16
    o, i_ = iota((2 * m, 2 * m), 0), iota((2 * m, 2 * m), 1)
    rest = mod(o, m)
    from_ = mod(div(rest, 8), 2) * m + div(rest, 16) * 16 + div(o, m) * 8 + mod(rest, 8)
    order = jnp.where(i_ == from_, 1.0, 0.0).astype(BF16)
    lab_y[0]()

    for load in loads[4:]:
        load.wait()
    pool_n = pool.shape[0]
    emb[0:pool_n, :] = unit_rows(pool[...].astype(F32))

    def pass_on(h, other):
        g = G.at[c, h, other]
        remote(g, g, ws.at[h, other], wr.at[h, other], ring[h](other)).wait_recv()
        to_sibling(h, other).start()

    def arrange(h, i):
        g = G.at[1 - c, h, i]
        remote(g, g, sibs.at[h, i], sibr.at[h, i], sibling).wait_recv()
        pair = jnp.concatenate([G[0, h, i].reshape(m, hh), G[1, h, i].reshape(m, hh)], axis=0)
        w = mm(order, pair).astype(BF16)
        cols = slice(h * hh, (h + 1) * hh)
        for ref, part in ((up, w[:m]), (down, w[m:])):
            if h == 0:
                for zz in range(n):
                    at = pl.multiple_of((zz * n + i) * 16, 16)
                    ref[pl.ds(at, 16), cols] = part[zz * 16 : (zz + 1) * 16]
            else:
                ref[pl.ds(pl.multiple_of(i * m, m), m), cols] = part

    def arrange_at(k):
        for h in range(2):
            arrange(h, (place[h] + k) % n)
            arrange(h, (place[h] + n - k) % n)

    def pass_on_at(k):
        for h in range(2):
            pass_on(h, (place[h] + k) % n)
            pass_on(h, (place[h] + n - k) % n)

    if n > 2:
        pass_on_at(1)
    arrange(0, y)
    arrange(1, z)

    @pl.loop(2, n // 2)
    def _(k):
        pass_on_at(k)
        arrange_at(k - 1)

    for h in range(2):
        pass_on(h, (place[h] + n // 2) % n)
    if n > 2:
        arrange_at(n // 2 - 1)
    for h in range(2):
        arrange(h, (place[h] + n // 2) % n)

    def ffn(block):
        pre = mm(block, up[...]) + bias[...].astype(F32).reshape(1, up.shape[1])
        hidden = (0.5 * pre * (1.0 + lax.erf(pre * (0.5**0.5)))).astype(BF16)
        return mm_nt(hidden, down[...])

    half = toks // 2
    lo, hi = pl.ds(0, half), pl.ds(half, half)
    sums = []

    def give(j, rows_, dst, to):
        k = len(sums)
        sums.append(remote(PS.at[j, rows_], dst, qs.at[k], qr.at[k], (me, to)))
        sums[-1].start()

    t_send[2].wait_recv()
    PS[2] = ffn(T[2]).astype(BF16)
    give(2, lo, RF.at[0], xp)
    give(2, hi, RF.at[1], xm)
    t_send[1].wait_recv()
    right = ffn(T[1])
    PS[1, hi] = right[half:].astype(BF16)
    give(1, hi, RA.at[0, hi], xp)
    t_send[0].wait_recv()
    left = ffn(T[0])
    PS[0, lo] = left[:half].astype(BF16)
    give(0, lo, RA.at[1, lo], xm)
    lab_y[1]()
    TL[...] = mm(by_z, RL[...].reshape(total, LAB)).astype(BF16).reshape(n, 2 * nyc, LAB)
    lab_z[0]()

    sums[0].wait_recv()
    PS[1, lo] = (right[:half] + RF[0].astype(F32)).astype(BF16)
    give(1, lo, RA.at[0, lo], xp)
    sums[1].wait_recv()
    PS[0, hi] = (left[half:] + RF[1].astype(F32)).astype(BF16)
    give(0, hi, RA.at[1, hi], xm)
    state = tok[...].astype(F32) + ffn(tok[...])
    for q in sums[2:]:
        q.wait_recv()
    state = state + RA[0].astype(F32) + RA[1].astype(F32)

    mean = jnp.mean(state, axis=1, keepdims=True)
    centred = state - mean
    var = jnp.mean(centred * centred, axis=1, keepdims=True)
    normed = centred * lax.rsqrt(var + 1e-05) * gain[...]
    docs = lengths.shape[1]
    len_row = lengths[...].astype(F32)
    len_col = to_column(len_row, docs)
    upto = iota((docs, docs), 1) <= iota((docs, docs), 0)
    ends = jnp.sum(jnp.where(upto, len_row, 0.0), axis=1, keepdims=True)
    places = iota((docs, toks), 1).astype(F32)
    member = jnp.where((places >= ends - len_col) & (places < ends), 1.0, 0.0)
    pooled = (
        jnp.dot(member, normed, precision=lax.Precision.HIGHEST, preferred_element_type=F32)
        / len_col
    )
    emb[pool_n : pool_n + docs, :] = unit_rows(pooled)

    w = d // 4
    p_y = [exchange(SP.at[k], RP.at[k], yc, nyc, at_yc, yps.at[k], ypr.at[k]) for k in range(2)]
    p_z = [exchange(TP.at[k], FP.at[k], z, n, at_z, zps.at[k], zpr.at[k]) for k in range(2)]
    q_z = [exchange(SQ.at[k], RQ.at[k], z, n, at_z, zqs.at[k], zqr.at[k]) for k in range(2)]
    q_y = [exchange(TQ.at[k], FQ.at[k], yc, nyc, at_yc, yqs.at[k], yqr.at[k]) for k in range(2)]
    for k in range(2):
        e0 = emb[:, 2 * k * w : (2 * k + 1) * w]
        e1 = emb[:, (2 * k + 1) * w : (2 * k + 2) * w]
        SP[k] = mm(pick0, e0).astype(BF16).reshape(nyc, 2 * n, w)
        p_y[k][0]()
        SQ[k] = mm(pick1, e1).astype(BF16).reshape(n, 2 * nyc, w)
        q_z[k][0]()
    lab_z[1]()
    lx = [
        remote(L.at[0], L.at[1], lxs.at[0], lxr.at[0], (me, xp)),
        remote(L.at[0], L.at[2], lxs.at[1], lxr.at[1], (me, xm)),
    ]
    for t in lx:
        t.start()
    for k in range(2):
        p_y[k][1]()
        TP[k] = mm(by_z, RP[k].reshape(total, w)).astype(BF16).reshape(n, 2 * nyc, w)
        p_z[k][0]()
        q_z[k][1]()
        TQ[k] = mm(by_yc, RQ[k].reshape(total, w)).astype(BF16).reshape(nyc, 2 * n, w)
        q_y[k][0]()

    xs = []
    for k in range(2):
        p_z[k][1]()
        E[0, k, :, :w] = FP[k].reshape(total, w)
        q_y[k][1]()
        E[0, k, :, w:] = mm(by_z, FQ[k].reshape(total, w)).astype(BF16)
        xs.append(remote(E.at[0, k], E.at[1, k], es.at[0, k], er.at[0, k], (me, xp)))
        xs.append(remote(E.at[0, k], E.at[2, k], es.at[1, k], er.at[1, k], (me, xm)))
        xs[-2].start()
        xs[-1].start()

    for t in lx:
        t.wait_recv()

    def labels(i):
        column = L[i].reshape(total, LAB)[:, 0:1].astype(F32)
        return column, jnp.sum(jnp.where(eye, column, 0.0), axis=0, keepdims=True)

    (col0, row0), (col1, row1), (col2, _) = labels(0), labels(1), labels(2)

    def part(j, i, k):
        return mm_nt(E[j, k], E[i, k])

    def best_of(sc, keep):
        return jnp.max(jnp.where(keep, sc, -1.0), axis=0, keepdims=True)

    best = best_of(part(0, 0, 0) + part(0, 0, 1), (col0 == row0) & ~eye)
    xs[0].wait_recv()
    xs[1].wait_recv()
    s21, s10, s20 = part(2, 1, 0), part(1, 0, 0), part(2, 0, 0)
    xs[2].wait_recv()
    xs[3].wait_recv()
    B1[1] = jnp.broadcast_to(best_of(s21 + part(2, 1, 1), col2 == row1), B1.shape[1:])
    over = B1.at[1, pl.ds(0, 1)]

    @pl.loop(0, n)
    def _(zz):
        remote(over, BM.at[z], bms.at[zz], bmr.at[z], (zz * nyc + yc, xm)).start()

    best = jnp.maximum(best, best_of(s10 + part(1, 0, 1), col1 == row0))
    best = jnp.maximum(best, best_of(s20 + part(2, 0, 1), col2 == row0))
    B1[0] = jnp.broadcast_to(best, B1.shape[1:])

    back_z = exchange(B1.at[0, pl.ds(0, 1)], B2, z, n, at_z, b1s, b1r, spread=True)
    back_z[0]()

    @pl.loop(0, n)
    def _(zz):
        remote(over, BM.at[zz], bms.at[zz], bmr.at[zz], (zz * nyc + yc, xm)).wait()

    back_z[1]()
    both_ = jnp.maximum(B2[...], BM[...]).reshape(n, total)
    LR[...] = pltpu.roll(both_, (total - z * 2 * nyc) % total, 1)[:, : LR.shape[1]]
    back_y = exchange(LR, B3, yc, nyc, at_yc, b2s, b2r, spread=True)
    back_y[0]()
    back_y[1]()
    got = B3[...].reshape(dp, LR.shape[1])
    lane = iota(got.shape, 1)
    v0 = jnp.sum(jnp.where(lane == yc * 2, got, 0.0), axis=1, keepdims=True)
    v1 = jnp.sum(jnp.where(lane == yc * 2 + 1, got, 0.0), axis=1, keepdims=True)
    mine = iota((dp, rows), 0) == owner_at
    mine_best = jnp.where(mine, jnp.where(place_in == 0, v0, v1), 0.0)
    out[...] = jnp.sum(mine_best, axis=0, keepdims=True).reshape(rows)

    @pl.loop(1, n)
    def _(k):
        for h in range(2):
            first_hop(h, k).wait_send()
            second_hop(h, k).wait_send()

    @pl.loop(0, n)
    def _(i):
        to_sibling(0, i).wait_send()
        to_sibling(1, i).wait_send()

    for t in [*t_send, *sums, *lx, *xs]:
        t.wait_send()


ANY = pl.BlockSpec(memory_space=pl.ANY)


def on_device(n, nx, tokens, w_up, b_up, w_down, ln_gain, doc_lengths, pool_rows, cluster_ids):
    toks, d = tokens.shape
    hid = w_up.shape[1]
    hh = hid // 2
    rows = cluster_ids.shape[0]
    nyc = 2 * n
    dp = nyc * n
    total = 2 * dp
    w = d // 4
    keep = min(total, 128)

    def vm(*shape):
        return pltpu.VMEM(shape, BF16)

    def vf(*shape):
        return pltpu.VMEM(shape, F32)

    def two(*shape):
        return [pltpu.SemaphoreType.DMA(shape)] * 2

    return pl.pallas_call(
        functools.partial(kernel, n, nx),
        out_shape=jax.ShapeDtypeStruct((rows,), F32),
        in_specs=[ANY] * 8,
        out_specs=pl.BlockSpec(memory_space=pltpu.VMEM),
        scratch_shapes=[
            vm(toks, d),
            vm(*w_up.shape),
            vm(*w_up.shape),
            vm(hid),
            vf(1, d),
            pltpu.VMEM(doc_lengths.shape, jnp.int32),
            vm(*pool_rows.shape),
            pltpu.VMEM((1, rows), jnp.int32),
            vm(2, 16, hh),
            vm(2, 2, n, n, 16, hh),
            vm(3, toks, d),
            vm(d, hid),
            vm(d, hid),
            vm(3, toks, d),
            vm(2, toks, d),
            vm(2, toks // 2, d),
            vm(rows, d),
            vm(nyc, 2 * n, LAB),
            vm(nyc, 2 * n, LAB),
            vm(n, 2 * nyc, LAB),
            vm(3, n, 2 * nyc, LAB),
            vm(2, nyc, 2 * n, w),
            vm(2, nyc, 2 * n, w),
            vm(2, n, 2 * nyc, w),
            vm(2, n, 2 * nyc, w),
            vm(2, n, 2 * nyc, w),
            vm(2, n, 2 * nyc, w),
            vm(2, nyc, 2 * n, w),
            vm(2, nyc, 2 * n, w),
            vm(3, 2, total, 2 * w),
            vf(2, 8, total),
            vf(n, 1, total),
            vf(n, 1, total),
            vf(n, keep),
            vf(nyc, n, keep),
            pltpu.SemaphoreType.DMA((8,)),
            *two(2, n),
            *two(2, n),
            *two(2, n),
            *two(3),
            *two(6),
            *two(nyc),
            *two(n),
            *two(2),
            *two(2, nyc),
            *two(2, n),
            *two(2, n),
            *two(2, nyc),
            *two(2, 2),
            *two(n),
            *two(n),
            *two(nyc),
        ],
        compiler_params=pltpu.CompilerParams(
            collective_id=0, has_side_effects=True, vmem_limit_bytes=58 * 2**20
        ),
    )(
        tokens,
        w_up,
        w_down.T,
        b_up,
        ln_gain.reshape(1, d),
        doc_lengths,
        pool_rows,
        cluster_ids.reshape(1, rows),
    )


def solution(mesh):
    n = math.isqrt(mesh.shape["dp"] // 2)
    placed = (
        P(("dp", "split"), None),
        P("dp", "split"),
        P("split"),
        P("split", "dp"),
        P(),
        P(("dp", "split"), None),
        P(("dp", "split"), None),
        P(("dp", "split")),
    )
    return jax.shard_map(
        functools.partial(on_device, n, mesh.shape["split"]),
        mesh=mesh,
        in_specs=placed,
        out_specs=P(("dp", "split")),
        check_vma=False,
    )
```

```python
import functools
import math

import jax
import jax.numpy as jnp
from jax import lax
from jax.experimental import pallas as pl
from jax.experimental.pallas import tpu as pltpu
from jax.sharding import PartitionSpec as P

MESH = pl.DeviceIdType.MESH
F32, BF16 = jnp.float32, jnp.bfloat16
LAB = 128


def iota(shape, dim):
    return lax.broadcasted_iota(jnp.int32, shape, dim)


def div(a, k):
    return a >> (k.bit_length() - 1)


def mod(a, k):
    return a & (k - 1)


def mm(a, b):
    return jnp.dot(a, b, preferred_element_type=F32)


def mm_nt(a, b):
    return lax.dot_general(a, b, (((1,), (1,)), ((), ())), preferred_element_type=F32)


def unit_rows(v):
    return (v * lax.rsqrt(jnp.sum(v * v, axis=1, keepdims=True) + 1e-06)).astype(BF16)


def here(n):
    me = lax.axis_index("dp")
    return me, me // (2 * n), (me // 2) % n, me % 2, lax.axis_index("split")


def to_column(row, size):
    eye = iota((size, size), 0) == iota((size, size), 1)
    return jnp.sum(jnp.where(eye, row, 0.0), axis=1, keepdims=True)


def slots(ids_ref, n):
    dp = 2 * n * n
    rows = ids_ref.shape[1]
    ids = ids_ref[...]
    owner, label = mod(ids, dp), div(ids, dp)
    owner_col = to_column(owner.astype(F32), rows)
    same = owner_col == owner.astype(F32)
    before = iota((rows, rows), 0) < iota((rows, rows), 1)
    place = jnp.sum(jnp.where(same & before, 1.0, 0.0), axis=0, keepdims=True).astype(jnp.int32)
    return owner, place, to_column(label.astype(F32), rows)


def remote(src, dst, send, recv, dev):
    return pltpu.make_async_remote_copy(
        src_ref=src, dst_ref=dst, send_sem=send, recv_sem=recv, device_id=dev, device_id_type=MESH
    )


def exchange(src, dst, mine, count, dev, send, recv, spread=False):
    def piece(other):
        return src if spread else src.at[other]

    def start():
        @pl.loop(1, count)
        def _(k):
            other = (mine + k) % count
            remote(piece(other), dst.at[mine], send.at[other], recv.at[mine], dev(other)).start()

        dst[mine] = src[...] if spread else src[mine]

    def landing(k):
        other = (mine + k) % count
        return remote(piece(other), dst.at[other], send.at[other], recv.at[other], dev(other))

    def arrived():
        @pl.loop(1, count)
        def _(k):
            landing(k).wait_recv()

    def sent():
        @pl.loop(1, count)
        def _(k):
            landing(k).wait_send()

    return start, arrived, sent


def kernel(
    n, nx, tok_in, w_up_in, w_down_in, bias_in, gain_in, lengths_in, pool_in, ids_in, out,
    tok, w_up, w_down, bias, gain, lengths, pool, ids, shard, G, T, up, down, PS, RA, RF, emb,
    SL, RL, TL, L, SP, RP, TP, FP, SQ, RQ, TQ, FQ, E, B1, B2, BM, LR, B3,
    lsem, p1s, p1r, ws, wr, sibs, sibr, ts, tr, qs, qr,
    yls, ylr, zls, zlr, lxs, lxr, yps, ypr, zps, zpr, zqs, zqr, yqs, yqr, es, er,
    b1s, b1r, bms, bmr, b2s, b2r,
):
    me, z, y, c, x = here(n)
    nyc = 2 * n
    yc = me % nyc
    dp = nyc * n
    total = 2 * dp
    hh = shard.shape[2]
    toks, d = tok.shape
    rows = ids.shape[1]
    xp, xm, xo = (x + 1) % nx, (x + nx - 1) % nx, (x + 2) % nx

    def at_z(zz):
        return (zz * nyc + yc, x)

    def at_y(yy):
        return ((z * n + yy) * 2 + c, x)

    def at_yc(other):
        return (z * nyc + other, x)

    place = (y, z)
    ring = (at_y, at_z)
    first = (at_z, at_y)
    sibling = (me + 1 - 2 * c, x)

    barrier = pltpu.get_barrier_semaphore()

    def greet(dev):
        pl.semaphore_signal(barrier, 1, device_id=dev, device_id_type=MESH)

    for other in (xp, xm, xo):
        greet((me, other))
    greet(sibling)

    @pl.loop(1, n)
    def _(k):
        greet(at_z((z + k) % n))
        greet(at_y((y + k) % n))

    loads = [
        pltpu.make_async_copy(src, dst, lsem.at[k])
        for k, (src, dst) in enumerate(
            (
                (w_up_in, w_up),
                (w_down_in, w_down),
                (tok_in, tok),
                (ids_in, ids),
                (pool_in, pool),
                (bias_in, bias),
                (gain_in, gain),
                (lengths_in, lengths),
            )
        )
    ]
    for load in loads:
        load.start()
    for load in loads[:3]:
        load.wait()
    both = jnp.concatenate([w_up[...].astype(F32), w_down[...].astype(F32)], axis=0).astype(BF16)
    shard[0] = both[:, :hh]
    shard[1] = both[:, hh:]
    pl.semaphore_wait(barrier, 2 * (n - 1) + 4)

    def first_hop(h, k):
        mine = (z, y)[h]
        other = (mine + k) % n
        slot = G.at[c, 0, y, z] if h == 0 else G.at[c, 1, z, y]
        return remote(shard.at[h], slot, p1s.at[h, other], p1r.at[h, mine], first[h](other))

    @pl.loop(1, n)
    def _(k):
        first_hop(0, k).start()
        first_hop(1, k).start()

    t_send = [
        remote(tok, T.at[0], ts.at[0], tr.at[0], (me, xp)),
        remote(tok, T.at[1], ts.at[1], tr.at[1], (me, xm)),
        remote(tok, T.at[2], ts.at[2], tr.at[2], (me, xo)),
    ]
    for t in t_send:
        t.start()
    G[c, 0, y, z] = shard[0]
    G[c, 1, z, y] = shard[1]

    @pl.loop(1, n)
    def _(k):
        for h in range(2):
            mine = (z, y)[h]
            other = (mine + k) % n
            slot_ = G.at[c, 0, y, other] if h == 0 else G.at[c, 1, z, other]
            remote(shard.at[h], slot_, p1s.at[h, other], p1r.at[h, other], first[h](other)).wait_recv()

    def second_hop(h, k):
        q = place[h]
        other = (q + k) % n
        return remote(G.at[c, h, q], G.at[c, h, q], ws.at[h, other], wr.at[h, q], ring[h](other))

    def to_sibling(h, i):
        return remote(G.at[c, h, i], G.at[c, h, i], sibs.at[h, i], sibr.at[h, i], sibling)

    @pl.loop(1, n)
    def _(k):
        second_hop(0, k).start()
        second_hop(1, k).start()

    to_sibling(0, y).start()
    to_sibling(1, z).start()

    loads[3].wait()
    owner, place_in, label_col = slots(ids, n)
    slot = iota((total, rows), 0)
    owner_at = mod(owner, nyc) * n + div(owner, nyc)
    target0 = owner_at * 2 + place_in
    target1 = owner * 2 + place_in
    pick0 = jnp.where(slot == target0, 1.0, 0.0).astype(BF16)
    pick1 = jnp.where(slot == target1, 1.0, 0.0).astype(BF16)
    lab = jnp.broadcast_to(label_col + 1.0, (rows, LAB)).astype(BF16)
    SL[...] = mm(pick0, lab).astype(BF16).reshape(nyc, 2 * n, LAB)
    lab_y = exchange(SL, RL, yc, nyc, at_yc, yls, ylr)
    lab_z = exchange(TL, L.at[0], z, n, at_z, zls, zlr)

    row, col = iota((total, total), 0), iota((total, total), 1)
    eye = row == col
    s_ = mod(row, 2)
    from_ = (mod(div(row, 2), nyc) * n + div(row, 2 * nyc)) * 2 + s_
    by_z = jnp.where(col == from_, 1.0, 0.0).astype(BF16)
    from_ = (mod(div(row, 2), n) * nyc + div(row, 2 * n)) * 2 + s_
    by_yc = jnp.where(col == from_, 1.0, 0.0).astype(BF16)

    m = n * 16
    o, i_ = iota((2 * m, 2 * m), 0), iota((2 * m, 2 * m), 1)
    rest = mod(o, m)
    from_ = mod(div(rest, 8), 2) * m + div(rest, 16) * 16 + div(o, m) * 8 + mod(rest, 8)
    order = jnp.where(i_ == from_, 1.0, 0.0).astype(BF16)
    lab_y[0]()

    for load in loads[4:]:
        load.wait()
    pool_n = pool.shape[0]
    emb[0:pool_n, :] = unit_rows(pool[...].astype(F32))

    def pass_on(h, other):
        g = G.at[c, h, other]
        remote(g, g, ws.at[h, other], wr.at[h, other], ring[h](other)).wait_recv()
        to_sibling(h, other).start()

    def arrange(h, i):
        g = G.at[1 - c, h, i]
        remote(g, g, sibs.at[h, i], sibr.at[h, i], sibling).wait_recv()
        pair = jnp.concatenate([G[0, h, i].reshape(m, hh), G[1, h, i].reshape(m, hh)], axis=0)
        w = mm(order, pair).astype(BF16)
        cols = slice(h * hh, (h + 1) * hh)
        for ref, part in ((up, w[:m]), (down, w[m:])):
            if h == 0:
                for zz in range(n):
                    at = pl.multiple_of((zz * n + i) * 16, 16)
                    ref[pl.ds(at, 16), cols] = part[zz * 16 : (zz + 1) * 16]
            else:
                ref[pl.ds(pl.multiple_of(i * m, m), m), cols] = part

    def arrange_at(k):
        for h in range(2):
            arrange(h, (place[h] + k) % n)
            arrange(h, (place[h] + n - k) % n)

    def pass_on_at(k):
        for h in range(2):
            pass_on(h, (place[h] + k) % n)
            pass_on(h, (place[h] + n - k) % n)

    if n > 2:
        pass_on_at(1)
    arrange(0, y)
    arrange(1, z)

    @pl.loop(2, n // 2)
    def _(k):
        pass_on_at(k)
        arrange_at(k - 1)

    for h in range(2):
        pass_on(h, (place[h] + n // 2) % n)
    if n > 2:
        arrange_at(n // 2 - 1)
    for h in range(2):
        arrange(h, (place[h] + n // 2) % n)

    def ffn(block):
        pre = mm(block, up[...]) + bias[...].astype(F32).reshape(1, up.shape[1])
        hidden = (0.5 * pre * (1.0 + lax.erf(pre * (0.5**0.5)))).astype(BF16)
        return mm_nt(hidden, down[...])

    half = toks // 2
    lo, hi = pl.ds(0, half), pl.ds(half, half)
    sums = []

    def give(j, rows_, dst, to):
        k = len(sums)
        sums.append(remote(PS.at[j, rows_], dst, qs.at[k], qr.at[k], (me, to)))
        sums[-1].start()

    t_send[2].wait_recv()
    PS[2] = ffn(T[2]).astype(BF16)
    give(2, lo, RF.at[0], xp)
    give(2, hi, RF.at[1], xm)
    t_send[1].wait_recv()
    right = ffn(T[1])
    PS[1, hi] = right[half:].astype(BF16)
    t_send[0].wait_recv()
    left = ffn(T[0])
    PS[0, lo] = left[:half].astype(BF16)
    sums[0].wait_send()
    sums[1].wait_send()
    give(1, hi, RA.at[0, hi], xp)
    give(0, lo, RA.at[1, lo], xm)
    state = tok[...].astype(F32) + ffn(tok[...])
    sums[0].wait_recv()
    PS[1, lo] = (right[:half] + RF[0].astype(F32)).astype(BF16)
    give(1, lo, RA.at[0, lo], xp)
    sums[1].wait_recv()
    PS[0, hi] = (left[half:] + RF[1].astype(F32)).astype(BF16)
    give(0, hi, RA.at[1, hi], xm)

    lab_y[1]()
    TL[...] = mm(by_z, RL[...].reshape(total, LAB)).astype(BF16).reshape(n, 2 * nyc, LAB)
    lab_z[0]()

    for q in sums[2:]:
        q.wait_recv()
    state = state + RA[0].astype(F32) + RA[1].astype(F32)

    mean = jnp.mean(state, axis=1, keepdims=True)
    centred = state - mean
    var = jnp.mean(centred * centred, axis=1, keepdims=True)
    normed = centred * lax.rsqrt(var + 1e-05) * gain[...]
    docs = lengths.shape[1]
    len_row = lengths[...].astype(F32)
    len_col = to_column(len_row, docs)
    upto = iota((docs, docs), 1) <= iota((docs, docs), 0)
    ends = jnp.sum(jnp.where(upto, len_row, 0.0), axis=1, keepdims=True)
    places = iota((docs, toks), 1).astype(F32)
    member = jnp.where((places >= ends - len_col) & (places < ends), 1.0, 0.0)
    pooled = (
        jnp.dot(member, normed, precision=lax.Precision.HIGHEST, preferred_element_type=F32)
        / len_col
    )
    emb[pool_n : pool_n + docs, :] = unit_rows(pooled)

    w = d // 4
    p_y = [exchange(SP.at[k], RP.at[k], yc, nyc, at_yc, yps.at[k], ypr.at[k]) for k in range(2)]
    p_z = [exchange(TP.at[k], FP.at[k], z, n, at_z, zps.at[k], zpr.at[k]) for k in range(2)]
    q_z = [exchange(SQ.at[k], RQ.at[k], z, n, at_z, zqs.at[k], zqr.at[k]) for k in range(2)]
    q_y = [exchange(TQ.at[k], FQ.at[k], yc, nyc, at_yc, yqs.at[k], yqr.at[k]) for k in range(2)]
    for k in range(2):
        e0 = emb[:, 2 * k * w : (2 * k + 1) * w]
        e1 = emb[:, (2 * k + 1) * w : (2 * k + 2) * w]
        SQ[k] = mm(pick1, e1).astype(BF16).reshape(n, 2 * nyc, w)
        SP[k] = mm(pick0, e0).astype(BF16).reshape(nyc, 2 * n, w)
        if k:
            q_z[0][2]()
            p_y[0][2]()
        q_z[k][0]()
        p_y[k][0]()
    lab_z[1]()
    lx = [
        remote(L.at[0], L.at[1], lxs.at[0], lxr.at[0], (me, xp)),
        remote(L.at[0], L.at[2], lxs.at[1], lxr.at[1], (me, xm)),
    ]
    for t in lx:
        t.start()
    for k in range(2):
        q_z[k][1]()
        TQ[k] = mm(by_yc, RQ[k].reshape(total, w)).astype(BF16).reshape(nyc, 2 * n, w)
        q_y[k][0]()
        p_y[k][1]()
        TP[k] = mm(by_z, RP[k].reshape(total, w)).astype(BF16).reshape(n, 2 * nyc, w)
        p_z[k][0]()

    xs = []
    for k in range(2):
        p_z[k][1]()
        E[0, k, :, :w] = FP[k].reshape(total, w)
        q_y[k][1]()
        E[0, k, :, w:] = mm(by_z, FQ[k].reshape(total, w)).astype(BF16)
        xs.append(remote(E.at[0, k], E.at[1, k], es.at[0, k], er.at[0, k], (me, xp)))
        xs.append(remote(E.at[0, k], E.at[2, k], es.at[1, k], er.at[1, k], (me, xm)))
        xs[-2].start()
        xs[-1].start()

    for t in lx:
        t.wait_recv()

    def labels(i):
        column = L[i].reshape(total, LAB)[:, 0:1].astype(F32)
        return column, jnp.sum(jnp.where(eye, column, 0.0), axis=0, keepdims=True)

    (col0, row0), (col1, row1), (col2, _) = labels(0), labels(1), labels(2)

    def part(j, i, k):
        return mm_nt(E[j, k], E[i, k])

    def best_of(sc, keep):
        return jnp.max(jnp.where(keep, sc, -1.0), axis=0, keepdims=True)

    best = best_of(part(0, 0, 0) + part(0, 0, 1), (col0 == row0) & ~eye)
    xs[0].wait_recv()
    xs[1].wait_recv()
    s21, s10, s20 = part(2, 1, 0), part(1, 0, 0), part(2, 0, 0)
    xs[2].wait_recv()
    xs[3].wait_recv()
    B1[1] = jnp.broadcast_to(best_of(s21 + part(2, 1, 1), col2 == row1), B1.shape[1:])
    over = B1.at[1, pl.ds(0, 1)]

    @pl.loop(0, n)
    def _(zz):
        remote(over, BM.at[z], bms.at[zz], bmr.at[z], (zz * nyc + yc, xm)).start()

    best = jnp.maximum(best, best_of(s10 + part(1, 0, 1), col1 == row0))
    best = jnp.maximum(best, best_of(s20 + part(2, 0, 1), col2 == row0))
    B1[0] = jnp.broadcast_to(best, B1.shape[1:])

    back_z = exchange(B1.at[0, pl.ds(0, 1)], B2, z, n, at_z, b1s, b1r, spread=True)
    back_z[0]()

    @pl.loop(0, n)
    def _(zz):
        remote(over, BM.at[zz], bms.at[zz], bmr.at[zz], (zz * nyc + yc, xm)).wait()

    back_z[1]()
    both_ = jnp.maximum(B2[...], BM[...]).reshape(n, total)
    LR[...] = pltpu.roll(both_, (total - z * 2 * nyc) % total, 1)[:, : LR.shape[1]]
    back_y = exchange(LR, B3, yc, nyc, at_yc, b2s, b2r, spread=True)
    back_y[0]()
    back_y[1]()
    got = B3[...].reshape(dp, LR.shape[1])
    lane = iota(got.shape, 1)
    v0 = jnp.sum(jnp.where(lane == yc * 2, got, 0.0), axis=1, keepdims=True)
    v1 = jnp.sum(jnp.where(lane == yc * 2 + 1, got, 0.0), axis=1, keepdims=True)
    mine = iota((dp, rows), 0) == owner_at
    mine_best = jnp.where(mine, jnp.where(place_in == 0, v0, v1), 0.0)
    out[...] = jnp.sum(mine_best, axis=0, keepdims=True).reshape(rows)

    @pl.loop(1, n)
    def _(k):
        for h in range(2):
            first_hop(h, k).wait_send()
            second_hop(h, k).wait_send()

    @pl.loop(0, n)
    def _(i):
        to_sibling(0, i).wait_send()
        to_sibling(1, i).wait_send()

    for t in [*t_send, *sums[2:], *lx, *xs]:
        t.wait_send()
    for hop in (lab_y, lab_z, q_z[1], p_y[1], *q_y, *p_z, back_z, back_y):
        hop[2]()


ANY = pl.BlockSpec(memory_space=pl.ANY)


def on_device(n, nx, tokens, w_up, b_up, w_down, ln_gain, doc_lengths, pool_rows, cluster_ids):
    toks, d = tokens.shape
    hid = w_up.shape[1]
    hh = hid // 2
    rows = cluster_ids.shape[0]
    nyc = 2 * n
    dp = nyc * n
    total = 2 * dp
    w = d // 4
    keep = min(total, 128)

    def vm(*shape):
        return pltpu.VMEM(shape, BF16)

    def vf(*shape):
        return pltpu.VMEM(shape, F32)

    def two(*shape):
        return [pltpu.SemaphoreType.DMA(shape)] * 2

    return pl.pallas_call(
        functools.partial(kernel, n, nx),
        out_shape=jax.ShapeDtypeStruct((rows,), F32),
        in_specs=[ANY] * 8,
        out_specs=pl.BlockSpec(memory_space=pltpu.VMEM),
        scratch_shapes=[
            vm(toks, d),
            vm(*w_up.shape),
            vm(*w_up.shape),
            vm(hid),
            vf(1, d),
            pltpu.VMEM(doc_lengths.shape, jnp.int32),
            vm(*pool_rows.shape),
            pltpu.VMEM((1, rows), jnp.int32),
            vm(2, 16, hh),
            vm(2, 2, n, n, 16, hh),
            vm(3, toks, d),
            vm(d, hid),
            vm(d, hid),
            vm(3, toks, d),
            vm(2, toks, d),
            vm(2, toks // 2, d),
            vm(rows, d),
            vm(nyc, 2 * n, LAB),
            vm(nyc, 2 * n, LAB),
            vm(n, 2 * nyc, LAB),
            vm(3, n, 2 * nyc, LAB),
            vm(2, nyc, 2 * n, w),
            vm(2, nyc, 2 * n, w),
            vm(2, n, 2 * nyc, w),
            vm(2, n, 2 * nyc, w),
            vm(2, n, 2 * nyc, w),
            vm(2, n, 2 * nyc, w),
            vm(2, nyc, 2 * n, w),
            vm(2, nyc, 2 * n, w),
            vm(3, 2, total, 2 * w),
            vf(2, 8, total),
            vf(n, 1, total),
            vf(n, 1, total),
            vf(n, keep),
            vf(nyc, n, keep),
            pltpu.SemaphoreType.DMA((8,)),
            *two(2, n),
            *two(2, n),
            *two(2, n),
            *two(3),
            *two(6),
            *two(nyc),
            *two(n),
            *two(2),
            *two(2, nyc),
            *two(2, n),
            *two(2, n),
            *two(2, nyc),
            *two(2, 2),
            *two(n),
            *two(n),
            *two(nyc),
        ],
        compiler_params=pltpu.CompilerParams(
            collective_id=0, has_side_effects=True, vmem_limit_bytes=58 * 2**20
        ),
    )(
        tokens,
        w_up,
        w_down.T,
        b_up,
        ln_gain.reshape(1, d),
        doc_lengths,
        pool_rows,
        cluster_ids.reshape(1, rows),
    )


def solution(mesh):
    n = math.isqrt(mesh.shape["dp"] // 2)
    placed = (
        P(("dp", "split"), None),
        P("dp", "split"),
        P("split"),
        P("split", "dp"),
        P(),
        P(("dp", "split"), None),
        P(("dp", "split"), None),
        P(("dp", "split")),
    )
    return jax.shard_map(
        functools.partial(on_device, n, mesh.shape["split"]),
        mesh=mesh,
        in_specs=placed,
        out_specs=P(("dp", "split")),
        check_vma=False,
    )
```

```python
import functools
import math

import jax
import jax.numpy as jnp
from jax import lax
from jax.experimental import pallas as pl
from jax.experimental.pallas import tpu as pltpu
from jax.sharding import PartitionSpec as P

MESH = pl.DeviceIdType.MESH
F32, BF16 = jnp.float32, jnp.bfloat16
LAB = 128
KC = 4
NP = 4


def iota(shape, dim):
    return lax.broadcasted_iota(jnp.int32, shape, dim)


def div(a, k):
    return a >> (k.bit_length() - 1)


def mod(a, k):
    return a & (k - 1)


def mm(a, b):
    return jnp.dot(a, b, preferred_element_type=F32)


def mm_nt(a, b):
    return lax.dot_general(a, b, (((1,), (1,)), ((), ())), preferred_element_type=F32)


def unit_rows(v):
    return (v * lax.rsqrt(jnp.sum(v * v, axis=1, keepdims=True) + 1e-06)).astype(BF16)


def here(n):
    me = lax.axis_index("dp")
    return me, me // (2 * n), (me // 2) % n, me % 2, lax.axis_index("split")


def to_column(row, size):
    eye = iota((size, size), 0) == iota((size, size), 1)
    return jnp.sum(jnp.where(eye, row, 0.0), axis=1, keepdims=True)


def slots(ids_ref, n):
    dp = 2 * n * n
    rows = ids_ref.shape[1]
    ids = ids_ref[...]
    owner, label = mod(ids, dp), div(ids, dp)
    owner_col = to_column(owner.astype(F32), rows)
    same = owner_col == owner.astype(F32)
    before = iota((rows, rows), 0) < iota((rows, rows), 1)
    place = jnp.sum(jnp.where(same & before, 1.0, 0.0), axis=0, keepdims=True).astype(jnp.int32)
    return owner, place, to_column(label.astype(F32), rows)


def remote(src, dst, send, recv, dev):
    return pltpu.make_async_remote_copy(
        src_ref=src, dst_ref=dst, send_sem=send, recv_sem=recv, device_id=dev, device_id_type=MESH
    )


def exchange(src, dst, mine, count, dev, send, recv, spread=False):
    def piece(other):
        return src if spread else src.at[other]

    def start():
        @pl.loop(1, count)
        def _(k):
            other = (mine + k) % count
            remote(piece(other), dst.at[mine], send.at[other], recv.at[mine], dev(other)).start()

        dst[mine] = src[...] if spread else src[mine]

    def landing(k):
        other = (mine + k) % count
        return remote(piece(other), dst.at[other], send.at[other], recv.at[other], dev(other))

    def arrived():
        @pl.loop(1, count)
        def _(k):
            landing(k).wait_recv()

    def sent():
        @pl.loop(1, count)
        def _(k):
            landing(k).wait_send()

    return start, arrived, sent


def kernel(
    n, nx, tok_in, w_up_in, w_down_in, bias_in, gain_in, lengths_in, pool_in, ids_in, out,
    tok, w_up, w_down, bias, gain, lengths, pool, ids, shard, G, T, up, down, PS, RA, RF, emb,
    SL, RL, TL, L, SP, RP, TP, FP, SQ, RQ, TQ, FQ, E, B1, B2, BM, LR, B3,
    lsem, p1s, p1r, ws, wr, sibs, sibr, ts, tr, qs, qr,
    yls, ylr, zls, zlr, lxs, lxr, yps, ypr, zps, zpr, zqs, zqr, yqs, yqr, es, er,
    b1s, b1r, bms, bmr, b2s, b2r,
):
    me, z, y, c, x = here(n)
    nyc = 2 * n
    yc = me % nyc
    dp = nyc * n
    total = 2 * dp
    hh = shard.shape[2]
    toks, d = tok.shape
    rows = ids.shape[1]
    xp, xm, xo = (x + 1) % nx, (x + nx - 1) % nx, (x + 2) % nx

    def at_z(zz):
        return (zz * nyc + yc, x)

    def at_y(yy):
        return ((z * n + yy) * 2 + c, x)

    def at_yc(other):
        return (z * nyc + other, x)

    place = (y, z)
    ring = (at_y, at_z)
    first = (at_z, at_y)
    sibling = (me + 1 - 2 * c, x)

    barrier = pltpu.get_barrier_semaphore()

    def greet(dev):
        pl.semaphore_signal(barrier, 1, device_id=dev, device_id_type=MESH)

    for other in (xp, xm, xo):
        greet((me, other))
    greet(sibling)

    @pl.loop(1, n)
    def _(k):
        greet(at_z((z + k) % n))
        greet(at_y((y + k) % n))

    loads = [
        pltpu.make_async_copy(src, dst, lsem.at[k])
        for k, (src, dst) in enumerate(
            (
                (w_up_in, w_up),
                (w_down_in, w_down),
                (tok_in, tok),
                (ids_in, ids),
                (pool_in, pool),
                (bias_in, bias),
                (gain_in, gain),
                (lengths_in, lengths),
            )
        )
    ]
    for load in loads:
        load.start()
    for load in loads[:3]:
        load.wait()
    both = jnp.concatenate([w_up[...].astype(F32), w_down[...].astype(F32)], axis=0).astype(BF16)
    shard[0] = both[:, :hh]
    shard[1] = both[:, hh:]
    pl.semaphore_wait(barrier, 2 * (n - 1) + 4)

    def first_hop(h, k):
        mine = (z, y)[h]
        other = (mine + k) % n
        slot = G.at[c, 0, y, z] if h == 0 else G.at[c, 1, z, y]
        return remote(shard.at[h], slot, p1s.at[h, other], p1r.at[h, mine], first[h](other))

    @pl.loop(1, n)
    def _(k):
        first_hop(0, k).start()
        first_hop(1, k).start()

    t_send = [
        remote(tok, T.at[0], ts.at[0], tr.at[0], (me, xp)),
        remote(tok, T.at[1], ts.at[1], tr.at[1], (me, xm)),
        remote(tok, T.at[2], ts.at[2], tr.at[2], (me, xo)),
    ]
    for t in t_send:
        t.start()
    G[c, 0, y, z] = shard[0]
    G[c, 1, z, y] = shard[1]

    loads[3].wait()
    owner, place_in, label_col = slots(ids, n)
    slot = iota((total, rows), 0)
    owner_at = mod(owner, nyc) * n + div(owner, nyc)
    target0 = owner_at * 2 + place_in
    target1 = owner * 2 + place_in
    pick0 = jnp.where(slot == target0, 1.0, 0.0).astype(BF16)
    pick1 = jnp.where(slot == target1, 1.0, 0.0).astype(BF16)
    lab = jnp.broadcast_to(label_col + 1.0, (rows, LAB)).astype(BF16)
    SL[...] = mm(pick0, lab).astype(BF16).reshape(nyc, 2 * n, LAB)
    lab_y = exchange(SL, RL, yc, nyc, at_yc, yls, ylr)
    lab_z = exchange(TL, L.at[0], z, n, at_z, zls, zlr)

    row, col = iota((total, total), 0), iota((total, total), 1)
    eye = row == col
    s_ = mod(row, 2)
    from_ = (mod(div(row, 2), nyc) * n + div(row, 2 * nyc)) * 2 + s_
    by_z = jnp.where(col == from_, 1.0, 0.0).astype(BF16)
    from_ = (mod(div(row, 2), n) * nyc + div(row, 2 * n)) * 2 + s_
    by_yc = jnp.where(col == from_, 1.0, 0.0).astype(BF16)

    m = n * 16
    o, i_ = iota((2 * m, 2 * m), 0), iota((2 * m, 2 * m), 1)
    rest = mod(o, m)
    from_ = mod(div(rest, 8), 2) * m + div(rest, 16) * 16 + div(o, m) * 8 + mod(rest, 8)
    order = jnp.where(i_ == from_, 1.0, 0.0).astype(BF16)

    @pl.loop(1, n)
    def _(k):
        for h in range(2):
            mine = (z, y)[h]
            other = (mine + k) % n
            slot_ = G.at[c, 0, y, other] if h == 0 else G.at[c, 1, z, other]
            remote(shard.at[h], slot_, p1s.at[h, other], p1r.at[h, other], first[h](other)).wait_recv()

    def hop_of(h, row_, part_, sem, to):
        r = G.at[c, h, row_] if part_ is None else G.at[c, h, row_, pl.ds(part_ * (n // 2), n // 2)]
        rs = wr.at[h, n] if part_ == 1 else wr.at[h, row_]
        return remote(r, r, ws.at[h, sem], rs, ring[h](to))

    def around(h, k):
        return (place[h] + n + k) % n

    hops = []

    def go(h, row_, part_, sem, to):
        hops.append(hop_of(h, around(h, row_), part_, sem, around(h, to)))
        hops[-1].start()

    def to_sibling(h, i):
        return remote(G.at[c, h, i], G.at[c, h, i], sibs.at[h, i], sibr.at[h, i], sibling)

    for h in range(2):
        for k_, to in enumerate((2, -2, 1, -1)):
            go(h, 0, None, k_, to)

    to_sibling(0, y).start()
    to_sibling(1, z).start()

    def arrange(h, i):
        g = G.at[1 - c, h, i]
        remote(g, g, sibs.at[h, i], sibr.at[h, i], sibling).wait_recv()
        pair = jnp.concatenate([G[0, h, i].reshape(m, hh), G[1, h, i].reshape(m, hh)], axis=0)
        w = mm(order, pair).astype(BF16)
        cols = slice(h * hh, (h + 1) * hh)
        for ref, part in ((up, w[:m]), (down, w[m:])):
            if h == 0:
                for zz in range(n):
                    at = pl.multiple_of((zz * n + i) * 16, 16)
                    ref[pl.ds(at, 16), cols] = part[zz * 16 : (zz + 1) * 16]
            else:
                ref[pl.ds(pl.multiple_of(i * m, m), m), cols] = part

    def arrange_at(k):
        for h in range(2):
            arrange(h, (place[h] + k) % n)
            arrange(h, (place[h] + n - k) % n)

    def got(h, row_, part_=None):
        hop_of(h, around(h, row_), part_, 0, around(h, row_)).wait_recv()

    for h in range(2):
        got(h, -1)
        go(h, -1, None, 4, 2)
        got(h, 1)
        go(h, 1, None, 5, -2)
    for h in range(2):
        got(h, -2)
        go(h, -2, 0, 6, 2)
        got(h, 2)
        go(h, 2, 1, 7, -2)
    for h in range(2):
        for k in (1, -1, 2, -2):
            to_sibling(h, around(h, k)).start()

    lab_y[0]()

    for load in loads[4:]:
        load.wait()
    pool_n = pool.shape[0]
    emb[0:pool_n, :] = unit_rows(pool[...].astype(F32))

    arrange(0, y)
    arrange(1, z)
    arrange_at(1)
    arrange_at(2)
    for h in range(2):
        for k in (3, -3):
            got(h, k)
            to_sibling(h, around(h, k)).start()
    for h in range(2):
        got(h, n // 2, 0)
        got(h, n // 2, 1)
        to_sibling(h, around(h, n // 2)).start()
    arrange_at(3)
    for h in range(2):
        arrange(h, around(h, n // 2))

    def ffn(block):
        pre = mm(block, up[...]) + bias[...].astype(F32).reshape(1, up.shape[1])
        hidden = (0.5 * pre * (1.0 + lax.erf(pre * (0.5**0.5)))).astype(BF16)
        return mm_nt(hidden, down[...])

    half = toks // 2
    size = half // NP
    lo = [pl.ds(k * size, size) for k in range(NP)]
    hi = [pl.ds(half + k * size, size) for k in range(NP)]
    low, high = pl.ds(0, half), pl.ds(half, half)
    sums, final = [], []

    def give(j, rows_, dst, to):
        k = len(sums)
        sums.append(remote(PS.at[j, rows_], dst, qs.at[k], qr.at[k], (me, to)))
        sums[-1].start()
        return sums[-1]

    t_send[2].wait_recv()
    PS[2] = ffn(T[2]).astype(BF16)
    on_p, on_m = [], []
    for k in range(NP):
        on_p.append(give(2, lo[k], RF.at[0, lo[k]], xp))
        on_m.append(give(2, hi[k], RF.at[1, lo[k]], xm))
    t_send[1].wait_recv()
    right = ffn(T[1])
    t_send[0].wait_recv()
    left = ffn(T[0])
    PS[1, high] = right[half:].astype(BF16)
    PS[0, low] = left[:half].astype(BF16)
    final.append(give(1, high, RA.at[0, high], xp))
    final.append(give(0, low, RA.at[1, low], xm))
    state = tok[...].astype(F32) + ffn(tok[...])
    for k in range(NP):
        a, b = k * size, half + k * size
        on_p[k].wait_recv()
        PS[1, lo[k]] = (right[a : a + size] + RF[0, lo[k]].astype(F32)).astype(BF16)
        final.append(give(1, lo[k], RA.at[0, lo[k]], xp))
        on_m[k].wait_recv()
        PS[0, hi[k]] = (left[b : b + size] + RF[1, lo[k]].astype(F32)).astype(BF16)
        final.append(give(0, hi[k], RA.at[1, hi[k]], xm))

    lab_y[1]()
    TL[...] = mm(by_z, RL[...].reshape(total, LAB)).astype(BF16).reshape(n, 2 * nyc, LAB)
    lab_z[0]()

    for q in final:
        q.wait_recv()
    state = state + RA[0].astype(F32) + RA[1].astype(F32)

    mean = jnp.mean(state, axis=1, keepdims=True)
    centred = state - mean
    var = jnp.mean(centred * centred, axis=1, keepdims=True)
    normed = centred * lax.rsqrt(var + 1e-05) * gain[...]
    docs = lengths.shape[1]
    len_row = lengths[...].astype(F32)
    len_col = to_column(len_row, docs)
    upto = iota((docs, docs), 1) <= iota((docs, docs), 0)
    ends = jnp.sum(jnp.where(upto, len_row, 0.0), axis=1, keepdims=True)
    places = iota((docs, toks), 1).astype(F32)
    member = jnp.where((places >= ends - len_col) & (places < ends), 1.0, 0.0)
    pooled = (
        jnp.dot(member, normed, precision=lax.Precision.HIGHEST, preferred_element_type=F32)
        / len_col
    )
    emb[pool_n : pool_n + docs, :] = unit_rows(pooled)

    w = d // (2 * KC)
    p_y = [exchange(SP.at[k], RP.at[k], yc, nyc, at_yc, yps.at[k], ypr.at[k]) for k in range(KC)]
    p_z = [exchange(TP.at[k], FP.at[k], z, n, at_z, zps.at[k], zpr.at[k]) for k in range(KC)]
    q_z = [exchange(SQ.at[k], RQ.at[k], z, n, at_z, zqs.at[k], zqr.at[k]) for k in range(KC)]
    q_y = [exchange(TQ.at[k], FQ.at[k], yc, nyc, at_yc, yqs.at[k], yqr.at[k]) for k in range(KC)]
    for k in range(KC):
        e0 = emb[:, 2 * k * w : (2 * k + 1) * w]
        e1 = emb[:, (2 * k + 1) * w : (2 * k + 2) * w]
        SQ[k] = mm(pick1, e1).astype(BF16).reshape(n, 2 * nyc, w)
        SP[k] = mm(pick0, e0).astype(BF16).reshape(nyc, 2 * n, w)
        q_z[k][0]()
        p_y[k][0]()
    lab_z[1]()
    lx = [
        remote(L.at[0], L.at[1], lxs.at[0], lxr.at[0], (me, xp)),
        remote(L.at[0], L.at[2], lxs.at[1], lxr.at[1], (me, xm)),
    ]
    for t in lx:
        t.start()
    for k in range(KC):
        q_z[k][1]()
        TQ[k] = mm(by_yc, RQ[k].reshape(total, w)).astype(BF16).reshape(nyc, 2 * n, w)
        q_y[k][0]()
        p_y[k][1]()
        TP[k] = mm(by_z, RP[k].reshape(total, w)).astype(BF16).reshape(n, 2 * nyc, w)
        p_z[k][0]()

    xs = []
    for k in range(KC):
        p_z[k][1]()
        E[0, k, :, :w] = FP[k].reshape(total, w)
        q_y[k][1]()
        E[0, k, :, w:] = mm(by_z, FQ[k].reshape(total, w)).astype(BF16)
        xs.append(remote(E.at[0, k], E.at[1, k], es.at[0, k], er.at[0, k], (me, xp)))
        xs.append(remote(E.at[0, k], E.at[2, k], es.at[1, k], er.at[1, k], (me, xm)))
        xs[-2].start()
        xs[-1].start()

    for t in lx:
        t.wait_recv()

    def labels(i):
        column = L[i].reshape(total, LAB)[:, 0:1].astype(F32)
        return column, jnp.sum(jnp.where(eye, column, 0.0), axis=0, keepdims=True)

    (col0, row0), (col1, row1), (col2, _) = labels(0), labels(1), labels(2)

    def part(j, i, k):
        return mm_nt(E[j, k], E[i, k])

    def best_of(sc, keep):
        return jnp.max(jnp.where(keep, sc, -1.0), axis=0, keepdims=True)

    best = best_of(sum(part(0, 0, k) for k in range(KC)), (col0 == row0) & ~eye)
    s21, s10, s20 = [], [], []
    for k in range(KC):
        xs[2 * k].wait_recv()
        xs[2 * k + 1].wait_recv()
        s21.append(part(2, 1, k))
        if k < KC - 1:
            s10.append(part(1, 0, k))
            s20.append(part(2, 0, k))
    B1[1] = jnp.broadcast_to(best_of(sum(s21), col2 == row1), B1.shape[1:])
    over = B1.at[1, pl.ds(0, 1)]

    @pl.loop(0, n)
    def _(zz):
        remote(over, BM.at[z], bms.at[zz], bmr.at[z], (zz * nyc + yc, xm)).start()

    best = jnp.maximum(best, best_of(sum(s10) + part(1, 0, KC - 1), col1 == row0))
    best = jnp.maximum(best, best_of(sum(s20) + part(2, 0, KC - 1), col2 == row0))
    B1[0] = jnp.broadcast_to(best, B1.shape[1:])

    back_z = exchange(B1.at[0, pl.ds(0, 1)], B2, z, n, at_z, b1s, b1r, spread=True)
    back_z[0]()

    @pl.loop(0, n)
    def _(zz):
        remote(over, BM.at[zz], bms.at[zz], bmr.at[zz], (zz * nyc + yc, xm)).wait()

    back_z[1]()
    both_ = jnp.maximum(B2[...], BM[...]).reshape(n, total)
    LR[...] = pltpu.roll(both_, (total - z * 2 * nyc) % total, 1)[:, : LR.shape[1]]
    back_y = exchange(LR, B3, yc, nyc, at_yc, b2s, b2r, spread=True)
    back_y[0]()
    back_y[1]()
    got = B3[...].reshape(dp, LR.shape[1])
    lane = iota(got.shape, 1)
    v0 = jnp.sum(jnp.where(lane == yc * 2, got, 0.0), axis=1, keepdims=True)
    v1 = jnp.sum(jnp.where(lane == yc * 2 + 1, got, 0.0), axis=1, keepdims=True)
    mine = iota((dp, rows), 0) == owner_at
    mine_best = jnp.where(mine, jnp.where(place_in == 0, v0, v1), 0.0)
    out[...] = jnp.sum(mine_best, axis=0, keepdims=True).reshape(rows)

    @pl.loop(1, n)
    def _(k):
        for h in range(2):
            first_hop(h, k).wait_send()

    @pl.loop(0, n)
    def _(i):
        to_sibling(0, i).wait_send()
        to_sibling(1, i).wait_send()

    for t in [*hops, *t_send, *sums, *lx, *xs]:
        t.wait_send()
    for hop in (lab_y, lab_z, *q_z, *p_y, *q_y, *p_z, back_z, back_y):
        hop[2]()


ANY = pl.BlockSpec(memory_space=pl.ANY)


def on_device(n, nx, tokens, w_up, b_up, w_down, ln_gain, doc_lengths, pool_rows, cluster_ids):
    toks, d = tokens.shape
    hid = w_up.shape[1]
    hh = hid // 2
    rows = cluster_ids.shape[0]
    nyc = 2 * n
    dp = nyc * n
    total = 2 * dp
    w = d // (2 * KC)
    keep = min(total, 128)

    def vm(*shape):
        return pltpu.VMEM(shape, BF16)

    def vf(*shape):
        return pltpu.VMEM(shape, F32)

    def two(*shape):
        return [pltpu.SemaphoreType.DMA(shape)] * 2

    return pl.pallas_call(
        functools.partial(kernel, n, nx),
        out_shape=jax.ShapeDtypeStruct((rows,), F32),
        in_specs=[ANY] * 8,
        out_specs=pl.BlockSpec(memory_space=pltpu.VMEM),
        scratch_shapes=[
            vm(toks, d),
            vm(*w_up.shape),
            vm(*w_up.shape),
            vm(hid),
            vf(1, d),
            pltpu.VMEM(doc_lengths.shape, jnp.int32),
            vm(*pool_rows.shape),
            pltpu.VMEM((1, rows), jnp.int32),
            vm(2, 16, hh),
            vm(2, 2, n, n, 16, hh),
            vm(3, toks, d),
            vm(d, hid),
            vm(d, hid),
            vm(3, toks, d),
            vm(2, toks, d),
            vm(2, toks // 2, d),
            vm(rows, d),
            vm(nyc, 2 * n, LAB),
            vm(nyc, 2 * n, LAB),
            vm(n, 2 * nyc, LAB),
            vm(3, n, 2 * nyc, LAB),
            vm(KC, nyc, 2 * n, w),
            vm(KC, nyc, 2 * n, w),
            vm(KC, n, 2 * nyc, w),
            vm(KC, n, 2 * nyc, w),
            vm(KC, n, 2 * nyc, w),
            vm(KC, n, 2 * nyc, w),
            vm(KC, nyc, 2 * n, w),
            vm(KC, nyc, 2 * n, w),
            vm(3, KC, total, 2 * w),
            vf(2, 8, total),
            vf(n, 1, total),
            vf(n, 1, total),
            vf(n, keep),
            vf(nyc, n, keep),
            pltpu.SemaphoreType.DMA((8,)),
            *two(2, n),
            *two(2, n + 1),
            *two(2, n),
            *two(3),
            *two(2 + 4 * NP),
            *two(nyc),
            *two(n),
            *two(2),
            *two(KC, nyc),
            *two(KC, n),
            *two(KC, n),
            *two(KC, nyc),
            *two(2, KC),
            *two(n),
            *two(n),
            *two(nyc),
        ],
        compiler_params=pltpu.CompilerParams(
            collective_id=0, has_side_effects=True, vmem_limit_bytes=58 * 2**20
        ),
    )(
        tokens,
        w_up,
        w_down.T,
        b_up,
        ln_gain.reshape(1, d),
        doc_lengths,
        pool_rows,
        cluster_ids.reshape(1, rows),
    )


def solution(mesh):
    n = math.isqrt(mesh.shape["dp"] // 2)
    placed = (
        P(("dp", "split"), None),
        P("dp", "split"),
        P("split"),
        P("split", "dp"),
        P(),
        P(("dp", "split"), None),
        P(("dp", "split"), None),
        P(("dp", "split")),
    )
    return jax.shard_map(
        functools.partial(on_device, n, mesh.shape["split"]),
        mesh=mesh,
        in_specs=placed,
        out_specs=P(("dp", "split")),
        check_vma=False,
    )
```

```python
import functools
import math

import jax
import jax.numpy as jnp
from jax import lax
from jax.experimental import pallas as pl
from jax.experimental.pallas import tpu as pltpu
from jax.sharding import PartitionSpec as P

MESH = pl.DeviceIdType.MESH
F32, BF16 = jnp.float32, jnp.bfloat16
LAB = 128
KC = 4
NP = 4


def iota(shape, dim):
    return lax.broadcasted_iota(jnp.int32, shape, dim)


def div(a, k):
    return a >> (k.bit_length() - 1)


def mod(a, k):
    return a & (k - 1)


def mm(a, b):
    return jnp.dot(a, b, preferred_element_type=F32)


def mm_nt(a, b):
    return lax.dot_general(a, b, (((1,), (1,)), ((), ())), preferred_element_type=F32)


def unit_rows(v):
    return (v * lax.rsqrt(jnp.sum(v * v, axis=1, keepdims=True) + 1e-06)).astype(BF16)


def here(n):
    me = lax.axis_index("dp")
    return me, me // (2 * n), (me // 2) % n, me % 2, lax.axis_index("split")


def to_column(row, size):
    eye = iota((size, size), 0) == iota((size, size), 1)
    return jnp.sum(jnp.where(eye, row, 0.0), axis=1, keepdims=True)


def slots(ids_ref, n):
    dp = 2 * n * n
    rows = ids_ref.shape[1]
    ids = ids_ref[...]
    owner, label = mod(ids, dp), div(ids, dp)
    owner_col = to_column(owner.astype(F32), rows)
    same = owner_col == owner.astype(F32)
    before = iota((rows, rows), 0) < iota((rows, rows), 1)
    place = jnp.sum(jnp.where(same & before, 1.0, 0.0), axis=0, keepdims=True).astype(jnp.int32)
    return owner, place, to_column(label.astype(F32), rows)


def remote(src, dst, send, recv, dev):
    return pltpu.make_async_remote_copy(
        src_ref=src, dst_ref=dst, send_sem=send, recv_sem=recv, device_id=dev, device_id_type=MESH
    )


def exchange(src, dst, mine, count, dev, send, recv, spread=False):
    def piece(other):
        return src if spread else src.at[other]

    def start():
        @pl.loop(1, count)
        def _(k):
            other = (mine + k) % count
            remote(piece(other), dst.at[mine], send.at[other], recv.at[mine], dev(other)).start()

        dst[mine] = src[...] if spread else src[mine]

    def landing(k):
        other = (mine + k) % count
        return remote(piece(other), dst.at[other], send.at[other], recv.at[other], dev(other))

    def arrived():
        @pl.loop(1, count)
        def _(k):
            landing(k).wait_recv()

    def sent():
        @pl.loop(1, count)
        def _(k):
            landing(k).wait_send()

    return start, arrived, sent


def kernel(
    n, nx, tok_in, w_up_in, w_down_in, bias_in, gain_in, lengths_in, pool_in, ids_in, out,
    tok, w_up, w_down, bias, gain, lengths, pool, ids, shard, G, T, up, down, PS, RA, RF, emb,
    SL, RL, TL, L, SP, RP, TP, FP, SQ, RQ, TQ, FQ, E, B1, B2, BM, LR, B3,
    lsem, p1s, p1r, ws, wr, sibs, sibr, ts, tr, qs, qr,
    yls, ylr, zls, zlr, lxs, lxr, yps, ypr, zps, zpr, zqs, zqr, yqs, yqr, es, er,
    b1s, b1r, bms, bmr, b2s, b2r,
):
    me, z, y, c, x = here(n)
    nyc = 2 * n
    yc = me % nyc
    dp = nyc * n
    total = 2 * dp
    hh = shard.shape[2]
    toks, d = tok.shape
    rows = ids.shape[1]
    xp, xm, xo = (x + 1) % nx, (x + nx - 1) % nx, (x + 2) % nx

    def at_z(zz):
        return (zz * nyc + yc, x)

    def at_y(yy):
        return ((z * n + yy) * 2 + c, x)

    def at_yc(other):
        return (z * nyc + other, x)

    place = (y, z)
    ring = (at_y, at_z)
    first = (at_z, at_y)
    sibling = (me + 1 - 2 * c, x)

    barrier = pltpu.get_barrier_semaphore()

    def greet(dev):
        pl.semaphore_signal(barrier, 1, device_id=dev, device_id_type=MESH)

    for other in (xp, xm, xo):
        greet((me, other))
    greet(sibling)

    @pl.loop(1, n)
    def _(k):
        greet(at_z((z + k) % n))
        greet(at_y((y + k) % n))

    loads = [
        pltpu.make_async_copy(src, dst, lsem.at[k])
        for k, (src, dst) in enumerate(
            (
                (w_up_in, w_up),
                (w_down_in, w_down),
                (tok_in, tok),
                (ids_in, ids),
                (pool_in, pool),
                (bias_in, bias),
                (gain_in, gain),
                (lengths_in, lengths),
            )
        )
    ]
    for load in loads:
        load.start()
    for load in loads[:3]:
        load.wait()
    both = jnp.concatenate([w_up[...].astype(F32), w_down[...].astype(F32)], axis=0).astype(BF16)
    shard[0] = both[:, :hh]
    shard[1] = both[:, hh:]
    pl.semaphore_wait(barrier, 2 * (n - 1) + 4)

    def first_hop(h, k):
        mine = (z, y)[h]
        other = (mine + k) % n
        slot = G.at[c, 0, y, z] if h == 0 else G.at[c, 1, z, y]
        return remote(shard.at[h], slot, p1s.at[h, other], p1r.at[h, mine], first[h](other))

    @pl.loop(1, n)
    def _(k):
        first_hop(0, k).start()
        first_hop(1, k).start()

    t_send = [
        remote(tok, T.at[0], ts.at[0], tr.at[0], (me, xp)),
        remote(tok, T.at[1], ts.at[1], tr.at[1], (me, xm)),
        remote(tok, T.at[2], ts.at[2], tr.at[2], (me, xo)),
    ]
    for t in t_send:
        t.start()
    G[c, 0, y, z] = shard[0]
    G[c, 1, z, y] = shard[1]

    loads[3].wait()
    owner, place_in, label_col = slots(ids, n)
    slot = iota((total, rows), 0)
    owner_at = mod(owner, nyc) * n + div(owner, nyc)
    target0 = owner_at * 2 + place_in
    target1 = owner * 2 + place_in
    pick0 = jnp.where(slot == target0, 1.0, 0.0).astype(BF16)
    pick1 = jnp.where(slot == target1, 1.0, 0.0).astype(BF16)
    lab = jnp.broadcast_to(label_col + 1.0, (rows, LAB)).astype(BF16)
    SL[...] = mm(pick0, lab).astype(BF16).reshape(nyc, 2 * n, LAB)
    lab_y = exchange(SL, RL, yc, nyc, at_yc, yls, ylr)
    lab_z = exchange(TL, L.at[0], z, n, at_z, zls, zlr)

    row, col = iota((total, total), 0), iota((total, total), 1)
    eye = row == col
    s_ = mod(row, 2)
    from_ = (mod(div(row, 2), nyc) * n + div(row, 2 * nyc)) * 2 + s_
    by_z = jnp.where(col == from_, 1.0, 0.0).astype(BF16)
    from_ = (mod(div(row, 2), n) * nyc + div(row, 2 * n)) * 2 + s_
    by_yc = jnp.where(col == from_, 1.0, 0.0).astype(BF16)

    m = n * 16
    o, i_ = iota((2 * m, 2 * m), 0), iota((2 * m, 2 * m), 1)
    rest = mod(o, m)
    from_ = mod(div(rest, 8), 2) * m + div(rest, 16) * 16 + div(o, m) * 8 + mod(rest, 8)
    order = jnp.where(i_ == from_, 1.0, 0.0).astype(BF16)

    @pl.loop(1, n)
    def _(k):
        for h in range(2):
            mine = (z, y)[h]
            other = (mine + k) % n
            slot_ = G.at[c, 0, y, other] if h == 0 else G.at[c, 1, z, other]
            remote(shard.at[h], slot_, p1s.at[h, other], p1r.at[h, other], first[h](other)).wait_recv()

    def hop_of(h, row_, part_, sem, to):
        r = G.at[c, h, row_] if part_ is None else G.at[c, h, row_, pl.ds(part_ * (n // 2), n // 2)]
        rs = wr.at[h, n] if part_ == 1 else wr.at[h, row_]
        return remote(r, r, ws.at[h, sem], rs, ring[h](to))

    def around(h, k):
        return (place[h] + n + k) % n

    hops = []

    def go(h, row_, part_, sem, to):
        hops.append(hop_of(h, around(h, row_), part_, sem, around(h, to)))
        hops[-1].start()

    def to_sibling(h, i):
        return remote(G.at[c, h, i], G.at[c, h, i], sibs.at[h, i], sibr.at[h, i], sibling)

    for h in range(2):
        for k_, to in enumerate((2, -2, 1, -1)):
            go(h, 0, None, k_, to)

    to_sibling(0, y).start()
    to_sibling(1, z).start()

    def arrange(h, i):
        g = G.at[1 - c, h, i]
        remote(g, g, sibs.at[h, i], sibr.at[h, i], sibling).wait_recv()
        pair = jnp.concatenate([G[0, h, i].reshape(m, hh), G[1, h, i].reshape(m, hh)], axis=0)
        w = mm(order, pair).astype(BF16)
        cols = slice(h * hh, (h + 1) * hh)
        for ref, part in ((up, w[:m]), (down, w[m:])):
            if h == 0:
                for zz in range(n):
                    at = pl.multiple_of((zz * n + i) * 16, 16)
                    ref[pl.ds(at, 16), cols] = part[zz * 16 : (zz + 1) * 16]
            else:
                ref[pl.ds(pl.multiple_of(i * m, m), m), cols] = part

    def arrange_at(k):
        for h in range(2):
            arrange(h, (place[h] + k) % n)
            arrange(h, (place[h] + n - k) % n)

    def got(h, row_, part_=None):
        hop_of(h, around(h, row_), part_, 0, around(h, row_)).wait_recv()

    for h in range(2):
        got(h, -1)
        go(h, -1, None, 4, 2)
        got(h, 1)
        go(h, 1, None, 5, -2)
    for h in range(2):
        got(h, -2)
        go(h, -2, 0, 6, 2)
        got(h, 2)
        go(h, 2, 1, 7, -2)
    for h in range(2):
        for k in (1, -1, 2, -2):
            to_sibling(h, around(h, k)).start()

    lab_y[0]()

    for load in loads[4:]:
        load.wait()
    pool_n = pool.shape[0]
    emb[0:pool_n, :] = unit_rows(pool[...].astype(F32))

    arrange(0, y)
    arrange(1, z)
    for h in range(2):
        for k in (3, -3):
            got(h, k)
            to_sibling(h, around(h, k)).start()
    for h in range(2):
        got(h, n // 2, 0)
        got(h, n // 2, 1)
        to_sibling(h, around(h, n // 2)).start()
    arrange_at(1)
    arrange_at(2)
    arrange_at(3)
    for h in range(2):
        arrange(h, around(h, n // 2))

    def ffn(block):
        pre = mm(block, up[...]) + bias[...].astype(F32).reshape(1, up.shape[1])
        hidden = (0.5 * pre * (1.0 + lax.erf(pre * (0.5**0.5)))).astype(BF16)
        return mm_nt(hidden, down[...])

    half = toks // 2
    size = half // NP
    lo = [pl.ds(k * size, size) for k in range(NP)]
    hi = [pl.ds(half + k * size, size) for k in range(NP)]
    low, high = pl.ds(0, half), pl.ds(half, half)
    sums, final = [], []

    def give(j, rows_, dst, to):
        k = len(sums)
        sums.append(remote(PS.at[j, rows_], dst, qs.at[k], qr.at[k], (me, to)))
        sums[-1].start()
        return sums[-1]

    t_send[2].wait_recv()
    PS[2] = ffn(T[2]).astype(BF16)
    on_p, on_m = [], []
    for k in range(NP):
        on_p.append(give(2, lo[k], RF.at[0, lo[k]], xp))
        on_m.append(give(2, hi[k], RF.at[1, lo[k]], xm))
    t_send[1].wait_recv()
    right = ffn(T[1])
    t_send[0].wait_recv()
    left = ffn(T[0])
    PS[1, high] = right[half:].astype(BF16)
    PS[0, low] = left[:half].astype(BF16)
    final.append(give(1, high, RA.at[0, high], xp))
    final.append(give(0, low, RA.at[1, low], xm))
    state = tok[...].astype(F32) + ffn(tok[...])
    for k in range(NP):
        a, b = k * size, half + k * size
        on_p[k].wait_recv()
        PS[1, lo[k]] = (right[a : a + size] + RF[0, lo[k]].astype(F32)).astype(BF16)
        final.append(give(1, lo[k], RA.at[0, lo[k]], xp))
        on_m[k].wait_recv()
        PS[0, hi[k]] = (left[b : b + size] + RF[1, lo[k]].astype(F32)).astype(BF16)
        final.append(give(0, hi[k], RA.at[1, hi[k]], xm))

    lab_y[1]()
    TL[...] = mm(by_z, RL[...].reshape(total, LAB)).astype(BF16).reshape(n, 2 * nyc, LAB)
    lab_z[0]()

    for q in final:
        q.wait_recv()
    state = state + RA[0].astype(F32) + RA[1].astype(F32)

    mean = jnp.mean(state, axis=1, keepdims=True)
    centred = state - mean
    var = jnp.mean(centred * centred, axis=1, keepdims=True)
    normed = centred * lax.rsqrt(var + 1e-05) * gain[...]
    docs = lengths.shape[1]
    len_row = lengths[...].astype(F32)
    len_col = to_column(len_row, docs)
    upto = iota((docs, docs), 1) <= iota((docs, docs), 0)
    ends = jnp.sum(jnp.where(upto, len_row, 0.0), axis=1, keepdims=True)
    places = iota((docs, toks), 1).astype(F32)
    member = jnp.where((places >= ends - len_col) & (places < ends), 1.0, 0.0)
    pooled = (
        jnp.dot(member, normed, precision=lax.Precision.HIGHEST, preferred_element_type=F32)
        / len_col
    )
    emb[pool_n : pool_n + docs, :] = unit_rows(pooled)

    w = d // (2 * KC)
    p_y = [exchange(SP.at[k], RP.at[k], yc, nyc, at_yc, yps.at[k], ypr.at[k]) for k in range(KC)]
    p_z = [exchange(TP.at[k], FP.at[k], z, n, at_z, zps.at[k], zpr.at[k]) for k in range(KC)]
    q_z = [exchange(SQ.at[k], RQ.at[k], z, n, at_z, zqs.at[k], zqr.at[k]) for k in range(KC)]
    q_y = [exchange(TQ.at[k], FQ.at[k], yc, nyc, at_yc, yqs.at[k], yqr.at[k]) for k in range(KC)]
    for k in range(KC):
        e0 = emb[:, 2 * k * w : (2 * k + 1) * w]
        e1 = emb[:, (2 * k + 1) * w : (2 * k + 2) * w]
        SQ[k] = mm(pick1, e1).astype(BF16).reshape(n, 2 * nyc, w)
        SP[k] = mm(pick0, e0).astype(BF16).reshape(nyc, 2 * n, w)
        q_z[k][0]()
        p_y[k][0]()
    lab_z[1]()
    lx = [
        remote(L.at[0], L.at[1], lxs.at[0], lxr.at[0], (me, xp)),
        remote(L.at[0], L.at[2], lxs.at[1], lxr.at[1], (me, xm)),
    ]
    for t in lx:
        t.start()
    for k in range(KC):
        q_z[k][1]()
        TQ[k] = mm(by_yc, RQ[k].reshape(total, w)).astype(BF16).reshape(nyc, 2 * n, w)
        q_y[k][0]()
        p_y[k][1]()
        TP[k] = mm(by_z, RP[k].reshape(total, w)).astype(BF16).reshape(n, 2 * nyc, w)
        p_z[k][0]()

    xs = []
    for k in range(KC):
        p_z[k][1]()
        E[0, k, :, :w] = FP[k].reshape(total, w)
        q_y[k][1]()
        E[0, k, :, w:] = mm(by_z, FQ[k].reshape(total, w)).astype(BF16)
        xs.append(remote(E.at[0, k], E.at[1, k], es.at[0, k], er.at[0, k], (me, xp)))
        xs.append(remote(E.at[0, k], E.at[2, k], es.at[1, k], er.at[1, k], (me, xm)))
        xs[-2].start()
        xs[-1].start()

    for t in lx:
        t.wait_recv()

    def labels(i):
        column = L[i].reshape(total, LAB)[:, 0:1].astype(F32)
        return column, jnp.sum(jnp.where(eye, column, 0.0), axis=0, keepdims=True)

    (col0, row0), (col1, row1), (col2, _) = labels(0), labels(1), labels(2)

    def part(j, i, k):
        return mm_nt(E[j, k], E[i, k])

    def best_of(sc, keep):
        return jnp.max(jnp.where(keep, sc, -1.0), axis=0, keepdims=True)

    best = best_of(sum(part(0, 0, k) for k in range(KC)), (col0 == row0) & ~eye)
    s21, s10, s20 = [], [], []
    for k in range(KC):
        xs[2 * k].wait_recv()
        xs[2 * k + 1].wait_recv()
        s21.append(part(2, 1, k))
        if k < KC - 1:
            s10.append(part(1, 0, k))
            s20.append(part(2, 0, k))
    B1[1] = jnp.broadcast_to(best_of(sum(s21), col2 == row1), B1.shape[1:])
    over = B1.at[1, pl.ds(0, 1)]

    @pl.loop(0, n)
    def _(zz):
        remote(over, BM.at[z], bms.at[zz], bmr.at[z], (zz * nyc + yc, xm)).start()

    best = jnp.maximum(best, best_of(sum(s10) + part(1, 0, KC - 1), col1 == row0))
    best = jnp.maximum(best, best_of(sum(s20) + part(2, 0, KC - 1), col2 == row0))
    B1[0] = jnp.broadcast_to(best, B1.shape[1:])

    back_z = exchange(B1.at[0, pl.ds(0, 1)], B2, z, n, at_z, b1s, b1r, spread=True)
    back_z[0]()

    @pl.loop(0, n)
    def _(zz):
        remote(over, BM.at[zz], bms.at[zz], bmr.at[zz], (zz * nyc + yc, xm)).wait()

    back_z[1]()
    both_ = jnp.maximum(B2[...], BM[...]).reshape(n, total)
    LR[...] = pltpu.roll(both_, (total - z * 2 * nyc) % total, 1)[:, : LR.shape[1]]
    back_y = exchange(LR, B3, yc, nyc, at_yc, b2s, b2r, spread=True)
    back_y[0]()
    back_y[1]()
    got = B3[...].reshape(dp, LR.shape[1])
    lane = iota(got.shape, 1)
    v0 = jnp.sum(jnp.where(lane == yc * 2, got, 0.0), axis=1, keepdims=True)
    v1 = jnp.sum(jnp.where(lane == yc * 2 + 1, got, 0.0), axis=1, keepdims=True)
    mine = iota((dp, rows), 0) == owner_at
    mine_best = jnp.where(mine, jnp.where(place_in == 0, v0, v1), 0.0)
    out[...] = jnp.sum(mine_best, axis=0, keepdims=True).reshape(rows)

    @pl.loop(1, n)
    def _(k):
        for h in range(2):
            first_hop(h, k).wait_send()

    @pl.loop(0, n)
    def _(i):
        to_sibling(0, i).wait_send()
        to_sibling(1, i).wait_send()

    for t in [*hops, *t_send, *sums, *lx, *xs]:
        t.wait_send()
    for hop in (lab_y, lab_z, *q_z, *p_y, *q_y, *p_z, back_z, back_y):
        hop[2]()


ANY = pl.BlockSpec(memory_space=pl.ANY)


def on_device(n, nx, tokens, w_up, b_up, w_down, ln_gain, doc_lengths, pool_rows, cluster_ids):
    toks, d = tokens.shape
    hid = w_up.shape[1]
    hh = hid // 2
    rows = cluster_ids.shape[0]
    nyc = 2 * n
    dp = nyc * n
    total = 2 * dp
    w = d // (2 * KC)
    keep = min(total, 128)

    def vm(*shape):
        return pltpu.VMEM(shape, BF16)

    def vf(*shape):
        return pltpu.VMEM(shape, F32)

    def two(*shape):
        return [pltpu.SemaphoreType.DMA(shape)] * 2

    return pl.pallas_call(
        functools.partial(kernel, n, nx),
        out_shape=jax.ShapeDtypeStruct((rows,), F32),
        in_specs=[ANY] * 8,
        out_specs=pl.BlockSpec(memory_space=pltpu.VMEM),
        scratch_shapes=[
            vm(toks, d),
            vm(*w_up.shape),
            vm(*w_up.shape),
            vm(hid),
            vf(1, d),
            pltpu.VMEM(doc_lengths.shape, jnp.int32),
            vm(*pool_rows.shape),
            pltpu.VMEM((1, rows), jnp.int32),
            vm(2, 16, hh),
            vm(2, 2, n, n, 16, hh),
            vm(3, toks, d),
            vm(d, hid),
            vm(d, hid),
            vm(3, toks, d),
            vm(2, toks, d),
            vm(2, toks // 2, d),
            vm(rows, d),
            vm(nyc, 2 * n, LAB),
            vm(nyc, 2 * n, LAB),
            vm(n, 2 * nyc, LAB),
            vm(3, n, 2 * nyc, LAB),
            vm(KC, nyc, 2 * n, w),
            vm(KC, nyc, 2 * n, w),
            vm(KC, n, 2 * nyc, w),
            vm(KC, n, 2 * nyc, w),
            vm(KC, n, 2 * nyc, w),
            vm(KC, n, 2 * nyc, w),
            vm(KC, nyc, 2 * n, w),
            vm(KC, nyc, 2 * n, w),
            vm(3, KC, total, 2 * w),
            vf(2, 8, total),
            vf(n, 1, total),
            vf(n, 1, total),
            vf(n, keep),
            vf(nyc, n, keep),
            pltpu.SemaphoreType.DMA((8,)),
            *two(2, n),
            *two(2, n + 1),
            *two(2, n),
            *two(3),
            *two(2 + 4 * NP),
            *two(nyc),
            *two(n),
            *two(2),
            *two(KC, nyc),
            *two(KC, n),
            *two(KC, n),
            *two(KC, nyc),
            *two(2, KC),
            *two(n),
            *two(n),
            *two(nyc),
        ],
        compiler_params=pltpu.CompilerParams(
            collective_id=0, has_side_effects=True, vmem_limit_bytes=58 * 2**20
        ),
    )(
        tokens,
        w_up,
        w_down.T,
        b_up,
        ln_gain.reshape(1, d),
        doc_lengths,
        pool_rows,
        cluster_ids.reshape(1, rows),
    )


def solution(mesh):
    n = math.isqrt(mesh.shape["dp"] // 2)
    placed = (
        P(("dp", "split"), None),
        P("dp", "split"),
        P("split"),
        P("split", "dp"),
        P(),
        P(("dp", "split"), None),
        P(("dp", "split"), None),
        P(("dp", "split")),
    )
    return jax.shard_map(
        functools.partial(on_device, n, mesh.shape["split"]),
        mesh=mesh,
        in_specs=placed,
        out_specs=P(("dp", "split")),
        check_vma=False,
    )
```
